128 devices in a mesh: dp: 8 (over y, core), expert: 16 (over x, z).
Axes of the slice: x: 4, y: 4, z: 4, core: 2. Of those that a mesh axis runs over, the one named last changes fastest.
Arguments:
- tokens: bfloat16 [16384, 2048], P(('dp', 'expert'))
- gain: float32 [2048], replicated, may hold values from 0.25 to 1.75
- gates: float32 [16384, 4], P(('dp', 'expert')), may hold values from 0.1 to 0.5
- expert_ids: int32 [16384, 4], P(('dp', 'expert')), may hold values from 0 to 127, as said below
- w_gate: bfloat16 [128, 2048, 768], P(('dp', 'expert')), may hold values from -0.125 to 0.125
- w_up: bfloat16 [128, 2048, 768], P(('dp', 'expert')), may hold values from -0.125 to 0.125
- w_down: bfloat16 [128, 768, 2048], P(('dp', 'expert')), may hold values from -0.21875 to 0.21875
- grad_out: bfloat16 [16384, 2048], P(('dp', 'expert'))
Outputs:
- moe_out: bfloat16 [16384, 2048], P(('dp', 'expert'))
- token_gradient: bfloat16 [16384, 2048], P(('dp', 'expert'))
- grad_gates: float32 [16384, 4], P(('dp', 'expert'))
- gain_gradient: float32 [2048], replicated
- grad_w_gate: bfloat16 [128, 2048, 768], P(('dp', 'expert'))
- grad_w_up: bfloat16 [128, 2048, 768], P(('dp', 'expert'))
- grad_w_down: bfloat16 [128, 768, 2048], P(('dp', 'expert'))
The draws below stay inside these ranges and needn't reach their ends.
Inputs may be any that keep to these rules, and one draw needn't show every extreme that they name: `expert_ids`: A token's 4 ids name distinct experts; the tokens of one device (aligned blocks of 128 rows) name no expert more than 8 times, and some expert exactly 8 times.
All inputs are finite; a program needn't handle non-finite values.
Results may differ from the reference program's by a relative error of at most 0.008.
Values may be sent and summed in bfloat16 or wider, within the bound.
A program may use at most 128 MiB of HBM per device.

```python
import math
import jax
import jax.numpy as jnp
from jax import lax

D = 2048
FF = 768
TOK_DEV = 128
TOP = 4
EXPERTS = 128
TOKENS = 16384
CAP = 8


def draw_tokens(key, part):
    key_base, key_row, key_col = jax.random.split(key, 3)
    base_values = jax.random.normal(key_base, (TOKENS, D), jnp.float32)
    row_scale = jnp.exp(jax.random.uniform(key_row, (TOKENS, 1), jnp.float32, math.log(0.3), math.log(3.0)))
    col_scale = jnp.exp(jax.random.uniform(key_col, (1, D), jnp.float32, math.log(0.3), math.log(3.0)))
    values = row_scale * col_scale * base_values
    return values.astype(jnp.bfloat16)


def draw_grad_out(key, part):
    key_base = jax.random.fold_in(key, 0)
    position = jnp.arange(TOKENS, dtype=jnp.float32)[:, None] / (TOKENS - 1)
    rising = 1.0 + 2.0 * position
    values = rising * jax.random.normal(key_base, (TOKENS, D), jnp.float32)
    return values.astype(jnp.bfloat16)


def draw_expert_ids(key, part):
    quarter = EXPERTS // 4
    step_size = CAP // 4
    hottest = jax.random.randint(jax.random.fold_in(key, 7), (), 0, EXPERTS).astype(jnp.int32)

    def block_ids(block_key):
        key_first, key_second, key_perm, key_rows = jax.random.split(block_key, 4)
        shift_first = jax.random.randint(key_first, (quarter,), 0, step_size + 1).astype(jnp.int32).at[0].set(0)
        shift_second = jax.random.randint(key_second, (quarter,), 0, step_size + 1).astype(jnp.int32)
        template = jnp.concatenate([CAP - shift_first, CAP // 2 - shift_second, step_size + shift_second, step_size + shift_first]).astype(jnp.int32)
        others = (hottest + 1 + jax.random.permutation(key_perm, EXPERTS - 1).astype(jnp.int32)) % EXPERTS
        ordering = jnp.concatenate([hottest[None], others]).astype(jnp.int32)
        counts = jnp.zeros((EXPERTS,), jnp.int32).at[ordering].set(template)
        bounds = jnp.cumsum(counts).astype(jnp.int32)
        listing = jnp.searchsorted(bounds, jnp.arange(TOK_DEV * TOP, dtype=jnp.int32), side='right').astype(jnp.int32)
        table = listing.reshape(TOP, TOK_DEV).T
        return table[jax.random.permutation(key_rows, TOK_DEV)]

    def block_key_of(index):
        return jax.random.fold_in(key, index + 11)
    block_keys = jax.vmap(block_key_of)(jnp.arange(TOKENS // TOK_DEV, dtype=jnp.int32))
    blocks = jax.vmap(block_ids)(block_keys)
    return blocks.reshape(TOKENS, TOP).astype(jnp.int32)


def levels(key, shape, shards, smallest, top_value):
    level = 1.0
    for dim, blocks in shards:
        steps = jax.random.uniform(jax.random.fold_in(jax.random.fold_in(key, 6), dim), (blocks,), jnp.float32, smallest / len(shards), top_value / len(shards))
        level = level * jnp.repeat(jnp.exp(steps), shape[dim] // blocks).reshape((-1,) + (1,) * (len(shape) - 1 - dim))
    return level


def noise(rng, extent, width, most, cuts=(), kind=jnp.bfloat16):
    loudness = levels(rng, extent, cuts, -0.22, 0.18) if cuts else 1.0
    entries = jax.random.normal(rng, extent, jnp.float32) * width * loudness
    return jnp.minimum(jnp.maximum(entries, -most), most).astype(kind)


def setup_inputs(seed: int = 0) -> dict:
    streams_of = jax.random.split(jax.random.key(seed), 9)
    return {
        "tokens": draw_tokens(jax.random.fold_in(streams_of[8], 71), 0),
        "gain": jnp.clip(1.0 + 0.15 * jax.random.normal(streams_of[1], (D,), jnp.float32), 0.25, 1.75),
        "gates": jnp.clip(jnp.exp(math.log(0.5) - 1.609438 * jax.random.uniform(streams_of[2], (TOKENS, TOP), jnp.float32) ** levels(streams_of[2], (TOKENS, TOP), ((0, 128),), -0.2, 0.2)), 0.1, 0.5),
        "expert_ids": draw_expert_ids(jax.random.fold_in(streams_of[8], 71), 0),
        "w_gate": noise(streams_of[4], (EXPERTS, D, FF), D ** -0.5, 0.125, ((0, 128),)),
        "w_up": noise(streams_of[5], (EXPERTS, D, FF), D ** -0.5, 0.125, ((0, 128),)),
        "w_down": noise(streams_of[6], (EXPERTS, FF, D), FF ** -0.5, 0.21875, ((0, 128),)),
        "grad_out": draw_grad_out(jax.random.fold_in(streams_of[8], 71), 0),
    }


def reference(tokens, gain, gates, expert_ids, w_gate, w_up, w_down, grad_out):
    widened_float = tokens.astype(jnp.float32)
    inverse_root_mean = lax.rsqrt(lax.optimization_barrier(jnp.mean(widened_float * widened_float, axis=1, keepdims=True)) + 1e-06)
    unit_scaled_input = widened_float * inverse_root_mean
    normalized_tokens = (unit_scaled_input * gain).astype(jnp.bfloat16)
    cotangent = grad_out.astype(jnp.float32)
    row_count = EXPERTS * CAP

    def per_expert(totals, expert_slot):
        out_sum, grad_sum, gate_grad = totals
        matches = expert_ids == expert_slot
        is_named = jnp.any(matches, axis=1)
        picked = jnp.nonzero(is_named, size=row_count, fill_value=0)[0].astype(jnp.int32)
        is_live = jnp.arange(row_count, dtype=jnp.int32) < jnp.sum(is_named.astype(jnp.int32))
        live_float = is_live.astype(jnp.float32)[:, None]
        chosen = matches[picked].astype(jnp.float32) * live_float
        route_gate = lax.optimization_barrier(jnp.sum(chosen * gates[picked], axis=1, keepdims=True))
        inputs = jnp.where(is_live[:, None], normalized_tokens[picked], jnp.zeros((), jnp.bfloat16))
        gate_matrix = w_gate[expert_slot]
        up_matrix = w_up[expert_slot]
        down_matrix = w_down[expert_slot]
        gate_pre = jnp.dot(inputs, gate_matrix, preferred_element_type=jnp.float32)
        up_pre = jnp.dot(inputs, up_matrix, preferred_element_type=jnp.float32)
        sigmoid_gate = jax.nn.sigmoid(gate_pre)
        act = (gate_pre * sigmoid_gate * up_pre).astype(jnp.bfloat16)
        expert_out = jnp.dot(act, down_matrix, preferred_element_type=jnp.float32).astype(jnp.bfloat16)
        out_float = expert_out.astype(jnp.float32)
        out_sum = out_sum.at[picked].add(route_gate * out_float)
        picked_grad = cotangent[picked]
        gate_grad = gate_grad.at[picked].add(chosen * lax.optimization_barrier(jnp.sum(picked_grad * out_float, axis=1, keepdims=True)))
        grad_route = (route_gate * picked_grad).astype(jnp.bfloat16)
        grad_act = jnp.dot(grad_route, down_matrix.T, preferred_element_type=jnp.float32)
        grad_gate_pre = (grad_act * up_pre * sigmoid_gate * (1.0 + gate_pre * (1.0 - sigmoid_gate))).astype(jnp.bfloat16)
        grad_up_pre = (grad_act * gate_pre * sigmoid_gate).astype(jnp.bfloat16)
        grad_down = jnp.dot(act.T, grad_route, preferred_element_type=jnp.float32).astype(jnp.bfloat16)
        grad_gate = jnp.dot(inputs.T, grad_gate_pre, preferred_element_type=jnp.float32).astype(jnp.bfloat16)
        grad_up = jnp.dot(inputs.T, grad_up_pre, preferred_element_type=jnp.float32).astype(jnp.bfloat16)
        partial_value = (jnp.dot(grad_gate_pre, gate_matrix.T, preferred_element_type=jnp.float32) + jnp.dot(grad_up_pre, up_matrix.T, preferred_element_type=jnp.float32)).astype(jnp.bfloat16)
        grad_sum = grad_sum.at[picked].add(partial_value.astype(jnp.float32))
        return ((out_sum, grad_sum, gate_grad), (grad_gate, grad_up, grad_down))
    start = (jnp.zeros((TOKENS, D), jnp.float32), jnp.zeros((TOKENS, D), jnp.float32), jnp.zeros((TOKENS, TOP), jnp.float32))
    totals, stacked = lax.scan(per_expert, start, jnp.arange(EXPERTS, dtype=jnp.int32))
    out_sum, normalized_gradient, grad_gates = totals
    grad_w_gate, grad_w_up, grad_w_down = stacked
    gain_gradient = lax.optimization_barrier(jnp.sum(normalized_gradient * unit_scaled_input, axis=0))
    scaled_tokens = normalized_gradient * gain
    token_gradient = (inverse_root_mean * (scaled_tokens - unit_scaled_input * lax.optimization_barrier(jnp.mean(scaled_tokens * unit_scaled_input, axis=1, keepdims=True)))).astype(jnp.bfloat16)
    return (out_sum.astype(jnp.bfloat16), token_gradient, grad_gates, gain_gradient, grad_w_gate, grad_w_up, grad_w_down)
```

```python
import functools

import jax
import jax.numpy as jnp
from jax import lax
from jax.experimental import pallas as pl
from jax.experimental.pallas import tpu as pltpu
from jax.sharding import PartitionSpec as P

MESH = pl.DeviceIdType.MESH
BF = jnp.bfloat16
F32 = jnp.float32
DEV = 128
CAP = 8
SLOTS = DEV * CAP
CHUNKS = 4
STEPS = DEV // CHUNKS
ROWS = STEPS * CAP
TILE = 256


def dot(left, right):
    return jnp.dot(left, right, preferred_element_type=F32)


def dot_nt(left, right):
    return lax.dot_general(left, right, (((1,), (1,)), ((), ())), preferred_element_type=F32)


def dot_tn(left, right):
    return lax.dot_general(left, right, (((0,), (0,)), ((), ())), preferred_element_type=F32)


def offsets_of(step):
    a, d, b, c = step % 4, (step // 4) % 4, (step // 16) % 4, step // 64
    return (a + b) % 4, c, a, (a + d) % 4


def device_at(step, dp, ex, sign):
    oy, oc, ox, oz = offsets_of(step)
    y, c, x, z = dp // 2, dp % 2, ex // 4, ex % 4
    return (
        ((y + sign * oy + 4) % 4) * 2 + (c + oc) % 2,
        ((x + sign * ox + 4) % 4) * 4 + (z + sign * oz + 4) % 4,
    )


def step_of(expert, dp, ex, sign):
    y, c, x, z = expert >> 5, (expert >> 4) & 1, (expert >> 2) & 3, expert & 3
    oy = (sign * (y - dp // 2)) & 3
    ox = (sign * (x - ex // 4)) & 3
    oz = (sign * (z - ex % 4)) & 3
    oc = (c + dp) & 1
    return ox + 4 * ((oz - ox) & 3) + 16 * ((oy - ox) & 3) + 64 * oc


def iota(shape, dim):
    return lax.broadcasted_iota(jnp.int32, shape, dim)


def kernel(
    tokens_ref, gain_ref, gates_ref, ids_ref, ids_t_ref, gates_t_ref, grad_out_ref, wg_hbm, wu_hbm, wd_hbm,
    moe_ref, tg_ref, gg_ref, ggain_ref, dwg_hbm, dwu_hbm, dwd_hbm,
    send_n, send_g, recv_n, recv_g, out_o, out_p, ret_o, ret_p,
    wg, wu, wd, act_s, dgp_s, dup_s, stage_g, stage_u, stage_d, slot_t, gain_sum, ring_a, ring_b,
    w_sem, s_sem, r_sem, st_sem, g_send, g_recv,
):
    tok, width = tokens_ref.shape
    dp, ex = lax.axis_index("dp"), lax.axis_index("expert")
    sign = 1 - 2 * (dp % 2)

    barrier = pltpu.get_barrier_semaphore()

    @pl.loop(1, DEV)
    def _(step):
        pl.semaphore_signal(barrier, inc=1, device_id=device_at(step, dp, ex, 1), device_id_type=MESH)

    loads = [
        pltpu.make_async_copy(src, dst, w_sem.at[j])
        for j, (src, dst) in enumerate(((wg_hbm, wg), (wu_hbm, wu), (wd_hbm, wd)))
    ]
    for load in loads:
        load.start()

    expert_row = iota((DEV, tok), 0)
    named = jnp.zeros((DEV, tok), F32)
    for k in range(4):
        named += (ids_t_ref[k : k + 1, :] == expert_row).astype(F32)
    earlier = (iota((tok, tok), 0) < iota((tok, tok), 1)).astype(BF)
    rank = dot(named.astype(BF), earlier)
    step_row = step_of(iota((SLOTS, DEV), 1), dp, ex, sign)
    spread = (step_row == (iota((SLOTS, DEV), 0) >> 3)).astype(BF)
    slot_rank = (iota((SLOTS, tok), 0) & 7).astype(F32)
    slots = jnp.where(dot(spread, rank.astype(BF)) == slot_rank, dot(spread, named.astype(BF)), 0.0)
    slots_b = slots.astype(BF)

    wide = tokens_ref[...].astype(F32)
    inverse = lax.rsqrt(jnp.mean(wide * wide, axis=1, keepdims=True) + 1e-06)
    normed = (wide * inverse * gain_ref[...]).astype(BF)

    gate_named = jnp.zeros((DEV, tok), F32)
    for k in range(4):
        gate_named += jnp.where(ids_t_ref[k : k + 1, :] == expert_row, gates_t_ref[k : k + 1, :], 0.0)
    gate_hi = gate_named.astype(BF)
    gate_mid = (gate_named - gate_hi.astype(F32)).astype(BF)
    gate_low = (gate_named - gate_hi.astype(F32) - gate_mid.astype(F32)).astype(BF)
    gate_all = dot(spread, gate_hi) + dot(spread, gate_mid) + dot(spread, gate_low)
    slot_gate = jnp.sum(gate_all * slots, axis=1, keepdims=True)

    for j in range(0, width, 512):
        part = dot(slots_b, normed[:, j : j + 512]).astype(BF).reshape(DEV, CAP, 512)
        send_n[:, :, j : j + 512] = part
        recv_n[0, :, j : j + 512] = part[0]

    pl.semaphore_wait(barrier, DEV - 1)

    def push(src, dst, kind, chunk, step, back):
        to = device_at(step, dp, ex, sign)
        if back:
            oc = offsets_of(step)[1]
            sender_sign = sign * (1 - 2 * oc)
            to = device_at(step, dp, ex, -sender_sign)
        pltpu.make_async_remote_copy(
            src_ref=src.at[step], dst_ref=dst.at[step], send_sem=s_sem.at[kind], recv_sem=r_sem.at[kind, chunk],
            device_id=to, device_id_type=MESH,
        ).start()

    def push_chunk(src, dst, kind, chunk, back):
        @pl.loop(jnp.where(chunk == 0, 1, 0), STEPS)
        def _(j):
            push(src, dst, kind, chunk, chunk * STEPS + j, back)

    def wait_chunk(dst, kind, chunk):
        if isinstance(chunk, int):
            first = 1 if chunk == 0 else 0
            view = dst.at[pl.ds(0, STEPS - first)]
            pltpu.make_async_copy(view, view, r_sem.at[kind, chunk]).wait()
            return

        @pl.when(chunk == 0)
        def _():
            view = dst.at[pl.ds(0, STEPS - 1)]
            pltpu.make_async_copy(view, view, r_sem.at[kind, 0]).wait()

        @pl.when(chunk > 0)
        def _():
            view = dst.at[pl.ds(0, STEPS)]
            pltpu.make_async_copy(view, view, r_sem.at[kind, chunk]).wait()

    push_chunk(send_n, recv_n, 0, 0, False)

    for j in range(0, width, 512):
        picked = dot(slots_b, grad_out_ref[:, j : j + 512])
        part = (picked * slot_gate).astype(BF).reshape(DEV, CAP, 512)
        send_g[:, :, j : j + 512] = part
        recv_g[0, :, j : j + 512] = part[0]

    push_chunk(send_g, recv_g, 1, 0, False)

    @pl.loop(1, CHUNKS)
    def _(chunk):
        push_chunk(send_n, recv_n, 0, chunk, False)
        push_chunk(send_g, recv_g, 1, chunk, False)

    expert_col = iota((tok, DEV), 1)
    named_t = jnp.zeros((tok, DEV), F32)
    gate_t = jnp.zeros((tok, DEV), F32)
    for k in range(4):
        hit = ids_ref[:, k : k + 1] == expert_col
        named_t += hit.astype(F32)
        gate_t += jnp.where(hit, gates_ref[:, k : k + 1], 0.0)
    later = (iota((tok, tok), 0) > iota((tok, tok), 1)).astype(BF)
    rank_t = dot(later, named_t.astype(BF))
    spread_t = (step_of(iota((DEV, SLOTS), 0), dp, ex, sign) == (iota((DEV, SLOTS), 1) >> 3)).astype(BF)
    live_t = jnp.where(
        dot(rank_t.astype(BF), spread_t) == (iota((tok, SLOTS), 1) & 7).astype(F32),
        dot(named_t.astype(BF), spread_t), 0.0,
    )
    gate_hi_t = gate_t.astype(BF)
    gate_low_t = (gate_t - gate_hi_t.astype(F32)).astype(BF)
    slot_t[0:tok, :] = (dot(gate_hi_t, spread_t) * live_t).astype(BF)
    slot_t[tok : 2 * tok, :] = (dot(gate_low_t, spread_t) * live_t).astype(BF)
    slot_t[2 * tok : 3 * tok, :] = live_t.astype(BF)

    for load in loads:
        load.wait()
    gain_sum[...] = jnp.zeros_like(gain_sum)

    @pl.loop(0, CHUNKS)
    def _(chunk):
        steps = pl.ds(chunk * STEPS, STEPS)
        rows = pl.ds(pl.multiple_of(chunk * ROWS, ROWS), ROWS)
        wait_chunk(recv_n, 0, chunk)
        inputs = recv_n[steps].reshape(ROWS, width)
        gate_pre = dot(inputs, wg[...])
        up_pre = dot(inputs, wu[...])
        sig = 1.0 / (1.0 + jnp.exp(-gate_pre))
        act = (gate_pre * sig * up_pre).astype(BF)
        act_s[rows, :] = act
        for j in range(0, width, 1024):
            out_o[steps, :, j : j + 1024] = dot(act, wd[:, j : j + 1024]).astype(BF).reshape(STEPS, CAP, 1024)

        @pl.when(chunk == 0)
        def _():
            ret_o[0] = out_o[0]

        push_chunk(out_o, ret_o, 2, chunk, True)
        wait_chunk(recv_g, 1, chunk)
        grad_act = dot_nt(recv_g[steps].reshape(ROWS, width), wd[...])
        dgp = (grad_act * up_pre * sig * (1.0 + gate_pre * (1.0 - sig))).astype(BF)
        dup = (grad_act * gate_pre * sig).astype(BF)
        dgp_s[rows, :] = dgp
        dup_s[rows, :] = dup
        for j in range(0, width, 1024):
            part = (dot_nt(dgp, wg[j : j + 1024, :]) + dot_nt(dup, wu[j : j + 1024, :])).astype(BF)
            out_p[steps, :, j : j + 1024] = part.reshape(STEPS, CAP, 1024)
            arrived = recv_n[steps, :, j : j + 1024].reshape(ROWS, 1024)
            gain_sum[:, j : j + 1024] += jnp.sum(part.astype(F32) * arrived.astype(F32), axis=0, keepdims=True)

        @pl.when(chunk == 0)
        def _():
            ret_p[0] = out_p[0]

        push_chunk(out_p, ret_p, 3, chunk, True)

    def exchange(ring, size, index, axis, sem, value):
        ring[index] = value

        @pl.loop(1, size)
        def _(j):
            pltpu.make_async_remote_copy(
                src_ref=ring.at[index], dst_ref=ring.at[index], send_sem=g_send.at[sem], recv_sem=g_recv.at[sem],
                device_id={axis: (index + j) % size}, device_id_type=MESH,
            ).start()

    def collect(ring, size, sem):
        view = ring.at[pl.ds(0, size - 1)]
        pltpu.make_async_copy(view, view, g_send.at[sem]).wait()
        pltpu.make_async_copy(view, view, g_recv.at[sem]).wait()
        total = ring[0]
        for j in range(1, size):
            total += ring[j]
        return total

    exchange(ring_a, 16, ex, "expert", 0, gain_sum[...] / gain_ref[...])

    def stage_copies(tile, slot):
        cols = pl.ds(pl.multiple_of(tile * TILE, TILE), TILE)
        return (
            pltpu.make_async_copy(stage_g.at[slot], dwg_hbm.at[cols], st_sem.at[0, slot]),
            pltpu.make_async_copy(stage_u.at[slot], dwu_hbm.at[cols], st_sem.at[1, slot]),
            pltpu.make_async_copy(stage_d.at[slot], dwd_hbm.at[:, cols], st_sem.at[2, slot]),
        )

    tiles = width // TILE

    @pl.loop(0, tiles)
    def _(tile):
        slot = tile % 2
        cols = pl.ds(pl.multiple_of(tile * TILE, TILE), TILE)

        @pl.when(tile >= 2)
        def _():
            for copy in stage_copies(tile - 2, slot):
                copy.wait()

        inputs = recv_n[:, :, cols].reshape(SLOTS, TILE)
        stage_g[slot] = dot_tn(inputs, dgp_s[...]).astype(BF)
        stage_u[slot] = dot_tn(inputs, dup_s[...]).astype(BF)
        stage_d[slot] = dot_tn(act_s[...], recv_g[:, :, cols].reshape(SLOTS, TILE)).astype(BF)
        for copy in stage_copies(tile, slot):
            copy.start()

    exchange(ring_b, 8, dp, "dp", 1, collect(ring_a, 16, 0))

    for chunk in range(CHUNKS):
        wait_chunk(ret_o, 2, chunk)
    for j in range(0, width, 512):
        both = dot(slot_t[0 : 2 * tok, :], ret_o[:, :, j : j + 512].reshape(SLOTS, 512))
        moe_ref[:, j : j + 512] = (both[0:tok] + both[tok : 2 * tok]).astype(BF)
    scores = dot_nt(grad_out_ref[...], ret_o[...].reshape(SLOTS, width)) * slot_t[2 * tok : 3 * tok, :].astype(F32)
    slot_step = iota((1, SLOTS), 1) >> 3
    oy, oc, ox, oz = offsets_of(slot_step)
    slot_expert = (
        32 * ((dp // 2 + sign * oy) & 3) + 16 * ((dp + oc) & 1)
        + 4 * ((ex // 4 + sign * ox) & 3) + ((ex % 4 + sign * oz) & 3)
    )
    for k in range(4):
        mine = jnp.where(ids_ref[:, k : k + 1] == slot_expert, scores, 0.0)
        gg_ref[:, k : k + 1] = jnp.sum(mine, axis=1, keepdims=True)

    ggain_ref[...] = collect(ring_b, 8, 1)

    for chunk in range(CHUNKS):
        wait_chunk(ret_p, 3, chunk)
    live = slot_t[2 * tok : 3 * tok, :]
    wide = tokens_ref[...].astype(F32)
    inverse = lax.rsqrt(jnp.mean(wide * wide, axis=1, keepdims=True) + 1e-06)
    xhat = wide * inverse
    scaled = dot(live, ret_p[...].reshape(SLOTS, width)) * gain_ref[...]
    mean = jnp.mean(scaled * xhat, axis=1, keepdims=True)
    tg_ref[...] = (inverse * (scaled - xhat * mean)).astype(BF)

    for tile in range(tiles - 2, tiles):
        for copy in stage_copies(tile, tile % 2):
            copy.wait()
    for kind, src in enumerate((send_n, send_g, out_o, out_p)):
        view = src.at[pl.ds(0, DEV - 1)]
        pltpu.make_async_copy(view, view, s_sem.at[kind]).wait()


def body(tokens, gain, gates, expert_ids, w_gate, w_up, w_down, grad_out):
    tok, width = tokens.shape
    hidden = w_gate.shape[2]
    vmem = pl.BlockSpec(memory_space=pltpu.VMEM)
    hbm = pl.BlockSpec(memory_space=pl.ANY)
    rows = pltpu.VMEM((DEV, CAP, width), BF)
    outs = pl.pallas_call(
        kernel,
        name="experts",
        out_shape=(
            jax.ShapeDtypeStruct((tok, width), BF),
            jax.ShapeDtypeStruct((tok, width), BF),
            jax.ShapeDtypeStruct((tok, 4), F32),
            jax.ShapeDtypeStruct((1, width), F32),
            jax.ShapeDtypeStruct((width, hidden), BF),
            jax.ShapeDtypeStruct((width, hidden), BF),
            jax.ShapeDtypeStruct((hidden, width), BF),
        ),
        in_specs=[vmem] * 7 + [hbm] * 3,
        out_specs=(vmem, vmem, vmem, vmem, hbm, hbm, hbm),
        scratch_shapes=[rows] * 8
        + [
            pltpu.VMEM((width, hidden), BF),
            pltpu.VMEM((width, hidden), BF),
            pltpu.VMEM((hidden, width), BF),
            pltpu.VMEM((SLOTS, hidden), BF),
            pltpu.VMEM((SLOTS, hidden), BF),
            pltpu.VMEM((SLOTS, hidden), BF),
            pltpu.VMEM((2, TILE, hidden), BF),
            pltpu.VMEM((2, TILE, hidden), BF),
            pltpu.VMEM((2, hidden, TILE), BF),
            pltpu.VMEM((3 * tok, SLOTS), BF),
            pltpu.VMEM((1, width), F32),
            pltpu.VMEM((16, 1, width), F32),
            pltpu.VMEM((8, 1, width), F32),
            pltpu.SemaphoreType.DMA((3,)),
            pltpu.SemaphoreType.DMA((4,)),
            pltpu.SemaphoreType.DMA((4, CHUNKS)),
            pltpu.SemaphoreType.DMA((3, 2)),
            pltpu.SemaphoreType.DMA((2,)),
            pltpu.SemaphoreType.DMA((2,)),
        ],
        compiler_params=pltpu.CompilerParams(
            collective_id=0, has_side_effects=True, vmem_limit_bytes=62 * 1024 * 1024
        ),
    )(
        tokens, gain[None], gates, expert_ids, expert_ids.T, gates.T, grad_out,
        w_gate[0], w_up[0], w_down[0],
    )
    moe_out, token_gradient, grad_gates, gain_gradient, grad_gate, grad_up, grad_down = outs
    return (
        moe_out, token_gradient, grad_gates, gain_gradient[0],
        grad_gate[None], grad_up[None], grad_down[None],
    )


def solution(mesh):
    both = P(("dp", "expert"), None)
    three = P(("dp", "expert"), None, None)
    return jax.shard_map(
        body,
        mesh=mesh,
        in_specs=(both, P(), both, both, three, three, three, both),
        out_specs=(both, both, both, P(), three, three, three),
        check_vma=False,
    )
```

```python
import jax
import jax.numpy as jnp
from jax import lax
from jax.experimental import pallas as pl
from jax.experimental.pallas import tpu as pltpu
from jax.sharding import PartitionSpec as P

MESH = pl.DeviceIdType.MESH
BF = jnp.bfloat16
F32 = jnp.float32
DEV = 128
CAP = 8
RING = 4
PLANE = 32
HALF = 16
TILE = 128
CUTS = (0, 640, 1280, 2048)
GROUPS = 3
PEERS = 73


def dot(left, right):
    return jnp.dot(left, right, preferred_element_type=F32)


def dot_nt(left, right):
    return lax.dot_general(left, right, (((1,), (1,)), ((), ())), preferred_element_type=F32)


def dot_tn(left, right):
    return lax.dot_general(left, right, (((0,), (0,)), ((), ())), preferred_element_type=F32)


def iota(shape, dim):
    return lax.broadcasted_iota(jnp.int32, shape, dim)


def cols(group):
    return pl.ds(CUTS[group], CUTS[group + 1] - CUTS[group])


def wide(group):
    return CUTS[group + 1] - CUTS[group]


def device(y, c, x, z):
    return y * 2 + c, x * 4 + z


def split(group, y, x, z):
    return ((x, y, z), (y, x, z), (z, x, y))[group]


def join(group, along, first, second):
    return ((first, along, second), (along, first, second), (second, first, along))[group]


def plane_offsets(step):
    return step % 4, (step % 4 + step // 4) % 4


def rows_of(ref, half, group, y, x, z):
    c = cols(group)
    if group == 0:
        return ref.at[half, y, :, z, :, c]
    if group == 1:
        return ref.at[half, :, x, z, :, c]
    return ref.at[half, y, x, :, :, c]


def kernel(
    tokens_ref, gain_ref, ids_ref, gates_ref, grad_out_ref, wg_hbm, wu_hbm, wd_hbm,
    moe_ref, tg_ref, gg_ref, ggain_ref, dwg_hbm, dwu_hbm, dwd_hbm,
    gn0, gn1, gn2, gg0, gg1, gg2,
    sn0, sn1, sn2, sg0, sg1, sg2, recv_n, recv_g, out_o, out_p,
    ro0, ro1, ro2, rp0, rp1, rp2, po0, po1, po2, pp0, pp1, pp2,
    wg, wu, wd, act_s, dgp_s, dup_s, stage_g, stage_u, stage_d,
    route, slot_s, gates_out, gates_in, gain_sum, ring_a, ring_b, inverse_s,
    w_sem, s_sem, r_sem, st_sem, g_send, g_recv, t_send, t_recv, m_send, m_recv, q_send, q_recv,
):
    tok, width = tokens_ref.shape
    gat_n, gat_g = (gn0, gn1, gn2), (gg0, gg1, gg2)
    send_n, send_g = (sn0, sn1, sn2), (sg0, sg1, sg2)
    ret_o, ret_p = (ro0, ro1, ro2), (rp0, rp1, rp2)
    par_o, par_p = (po0, po1, po2), (pp0, pp1, pp2)
    dp, ex = lax.axis_index("dp"), lax.axis_index("expert")
    y, c, x, z = dp // 2, dp % 2, ex // 4, ex % 4
    sign = 1 - 2 * c
    place = [split(g, y, x, z) for g in range(GROUPS)]

    barrier = pltpu.get_barrier_semaphore()

    @pl.loop(1, DEV)
    def _(step):
        oy, oc, ox, oz = step // 32, (step // 16) % 2, (step // 4) % 4, step % 4

        @pl.when(oy * ox * oz == 0)
        def _():
            pl.semaphore_signal(
                barrier, inc=1, device_id=device((y + oy) % 4, (c + oc) % 2, (x + ox) % 4, (z + oz) % 4),
                device_id_type=MESH,
            )

    loads = [
        pltpu.make_async_copy(src, dst, w_sem.at[j])
        for j, (src, dst) in enumerate(((wg_hbm, wg), (wu_hbm, wu), (wd_hbm, wd)))
    ]
    for load in loads:
        load.start()

    square_sum = jnp.zeros((tok, 1), F32)
    for g in range(GROUPS):
        part = tokens_ref[:, cols(g)].astype(F32)
        square_sum += jnp.sum(part * part, axis=1, keepdims=True)
    inverse_s[...] = lax.rsqrt(square_sum / width + 1e-06)
    own = jnp.concatenate([ids_ref[...].astype(F32), gates_ref[...]], axis=0)
    for g in range(GROUPS):
        along = place[g][0]
        route[g, along] = own
        xhat = tokens_ref[:, cols(g)].astype(F32) * inverse_s[...]
        gat_n[g][along] = (xhat * gain_ref[:, cols(g)]).astype(BF)
        gat_g[g][along] = grad_out_ref[:, cols(g)]

    pl.semaphore_wait(barrier, PEERS)

    def ring_device(g, along):
        yy, xx, zz = join(g, along, place[g][1], place[g][2])
        return device(yy, c, xx, zz)

    def around(start):
        for off in (1, 3, 2):
            for g in range(GROUPS):
                start(g, place[g][0], (place[g][0] + off) % 4)

    def remote(src, dst, send, recv, to):
        pltpu.make_async_remote_copy(
            src_ref=src, dst_ref=dst, send_sem=send, recv_sem=recv, device_id=to, device_id_type=MESH
        ).start()

    def await_bytes(view, sem):
        pltpu.make_async_copy(view, view, sem).wait()

    around(lambda g, me, to: remote(route.at[g, me], route.at[g, me], q_send.at[0], q_recv.at[0], ring_device(g, to)))
    for kind, gat in enumerate((gat_n, gat_g)):
        around(
            lambda g, me, to, kind=kind, gat=gat: remote(
                gat[g].at[me], gat[g].at[me], t_send.at[kind, g], t_recv.at[kind, g], ring_device(g, to)
            )
        )

    def plane_expert(g, rows):
        half, step = rows // HALF, rows % HALF
        first, second = plane_offsets(step)
        along, mine1, mine2 = place[g]
        yy, xx, zz = join(g, along, (mine1 + sign * first) & 3, (mine2 + sign * second) & 3)
        return 32 * yy + 16 * ((c + half) & 1) + 4 * xx + zz

    before = (iota((tok, tok), 0) < iota((tok, tok), 1)).astype(BF)

    def widen(rows):
        return jnp.broadcast_to(rows[:, None, :], (PLANE, CAP, tok)).reshape(PLANE * CAP, tok)

    await_bytes(route.at[:, pl.ds(0, 3)], q_recv.at[0])
    slot_rank = (iota((PLANE * CAP, tok), 0) & 7).astype(F32)
    for g in range(GROUPS):
        expert = plane_expert(g, iota((PLANE, tok), 0)).astype(F32)
        for p in range(RING):
            named = jnp.zeros((PLANE, tok), F32)
            gate = jnp.zeros((PLANE, tok), F32)
            for k in range(4):
                hit = route[g, p, k : k + 1, :] == expert
                named += hit.astype(F32)
                gate += jnp.where(hit, route[g, p, 4 + k : 5 + k, :], 0.0)
            rank = dot(named.astype(BF), before)
            live = jnp.where(widen(rank) == slot_rank, widen(named), 0.0)
            weight = live * widen(gate)
            high = weight.astype(BF)
            lanes = pl.ds(p * tok, tok)
            slot_s[g, 0, :, lanes] = live.astype(BF)
            slot_s[g, 1, :, lanes] = high
            slot_s[g, 2, :, lanes] = (weight - high.astype(F32)).astype(BF)

    def select(g, gat, send, recv, weighted):
        for p in range(RING):
            lanes = pl.ds(p * tok, tok)
            if weighted:
                picked = dot(slot_s[g, 1, :, lanes], gat[g][p]) + dot(slot_s[g, 2, :, lanes], gat[g][p])
            else:
                picked = dot(slot_s[g, 0, :, lanes], gat[g][p])
            picked = picked.astype(BF).reshape(PLANE, CAP, wide(g))
            send[g][:, p] = picked
            if g == 0:
                recv[0, y, p, z, :, cols(g)] = picked[0]
            elif g == 1:
                recv[0, p, x, z, :, cols(g)] = picked[0]
            else:
                recv[0, y, x, p, :, cols(g)] = picked[0]

    def push_out(send, recv, kind, half):
        @pl.loop(1 if half == 0 else 0, HALF)
        def _(step):
            first, second = plane_offsets(step)
            for g in range(GROUPS):
                along, mine1, mine2 = place[g]
                yy, xx, zz = join(g, along, (mine1 + sign * first + 4) % 4, (mine2 + sign * second + 4) % 4)
                remote(
                    send[g].at[half * HALF + step], rows_of(recv, half, g, y, x, z),
                    s_sem.at[kind, g], r_sem.at[kind, half, g], device(yy, (c + half) % 2, xx, zz),
                )

    def push_back(out, ret, kind, half):
        other = (c + half) % 2
        turn = 1 - 2 * other

        @pl.loop(jnp.where(half == 0, 1, 0), HALF)
        def _(step):
            first, second = plane_offsets(step)
            for g in range(GROUPS):
                along, mine1, mine2 = place[g]
                yy, xx, zz = join(g, along, (mine1 - turn * first + 4) % 4, (mine2 - turn * second + 4) % 4)
                remote(
                    rows_of(out, half, g, yy, xx, zz), ret[g].at[half * HALF + step],
                    s_sem.at[kind, g], r_sem.at[kind, half, g], device(yy, other, xx, zz),
                )

    def await_half(shape, kind, half):
        for g in range(GROUPS):
            if isinstance(half, int):
                await_bytes(shape[g].at[pl.ds(0, HALF - 1 + half)], r_sem.at[kind, half, g])
                continue

            @pl.when(half == 0)
            def _():
                await_bytes(shape[g].at[pl.ds(0, HALF - 1)], r_sem.at[kind, 0, g])

            @pl.when(half == 1)
            def _():
                await_bytes(shape[g].at[pl.ds(0, HALF)], r_sem.at[kind, 1, g])

    for g in range(GROUPS):
        await_bytes(gat_n[g].at[pl.ds(0, 3)], t_recv.at[0, g])
        select(g, gat_n, send_n, recv_n, False)
    push_out(send_n, recv_n, 0, 0)
    for g in range(GROUPS):
        await_bytes(gat_g[g].at[pl.ds(0, 3)], t_recv.at[1, g])
        select(g, gat_g, send_g, recv_g, True)
    push_out(send_g, recv_g, 1, 0)
    push_out(send_n, recv_n, 0, 1)
    push_out(send_g, recv_g, 1, 1)

    for load in loads:
        load.wait()
    gain_sum[...] = jnp.zeros_like(gain_sum)
    rows = PLANE // 2 * RING * CAP
    piece = rows // 2

    def keep(out, ret):
        for g in range(GROUPS):
            if g == 0:
                ret[g][0] = out[0, y, :, z, :, cols(g)]
            elif g == 1:
                ret[g][0] = out[0, :, x, z, :, cols(g)]
            else:
                ret[g][0] = out[0, y, x, :, :, cols(g)]

    @pl.loop(0, 4)
    def _(quarter):
        half, low = quarter // 2, quarter % 2
        span = pl.ds(pl.multiple_of(quarter * piece, piece), piece)
        lines = pl.ds(low * 2, 2)

        @pl.when(low == 0)
        def _():
            await_half(send_n, 0, half)
            await_half(send_g, 1, half)

        inputs = recv_n[half, lines].reshape(piece, width)
        gate_pre = dot(inputs, wg[...])
        up_pre = dot(inputs, wu[...])
        sig = 1.0 / (1.0 + jnp.exp(-gate_pre))
        act = (gate_pre * sig * up_pre).astype(BF)
        act_s[span, :] = act
        for j in range(0, width, 512):
            out_o[half, lines, :, :, :, j : j + 512] = (
                dot(act, wd[:, j : j + 512]).astype(BF).reshape(2, RING, RING, CAP, 512)
            )
        grad_act = dot_nt(recv_g[half, lines].reshape(piece, width), wd[...])
        dgp = (grad_act * up_pre * sig * (1.0 + gate_pre * (1.0 - sig))).astype(BF)
        dup = (grad_act * gate_pre * sig).astype(BF)
        dgp_s[span, :] = dgp
        dup_s[span, :] = dup
        for j in range(0, width, 512):
            part = (dot_nt(dgp, wg[j : j + 512, :]) + dot_nt(dup, wu[j : j + 512, :])).astype(BF)
            out_p[half, lines, :, :, :, j : j + 512] = part.reshape(2, RING, RING, CAP, 512)
            arrived = recv_n[half, lines, :, :, :, j : j + 512].reshape(piece, 512)
            gain_sum[:, j : j + 512] += jnp.sum(part.astype(F32) * arrived.astype(F32), axis=0, keepdims=True)

        @pl.when(quarter == 1)
        def _():
            keep(out_o, ret_o)
            keep(out_p, ret_p)

        @pl.when(low == 1)
        def _():
            push_back(out_o, ret_o, 2, half)
            push_back(out_p, ret_p, 3, half)

    def exchange(ring, size, index, axis, sem, value):
        ring[index] = value

        @pl.loop(1, size)
        def _(j):
            pltpu.make_async_remote_copy(
                src_ref=ring.at[index], dst_ref=ring.at[index], send_sem=g_send.at[sem], recv_sem=g_recv.at[sem],
                device_id={axis: (index + j) % size}, device_id_type=MESH,
            ).start()

    def collect(ring, size, sem):
        view = ring.at[pl.ds(0, size - 1)]
        await_bytes(view, g_send.at[sem])
        await_bytes(view, g_recv.at[sem])
        total = ring[0]
        for j in range(1, size):
            total += ring[j]
        return total

    exchange(ring_a, 16, ex, "expert", 0, gain_sum[...] / gain_ref[...])

    def stage_copies(tile, slot):
        span = pl.ds(pl.multiple_of(tile * TILE, TILE), TILE)
        return (
            pltpu.make_async_copy(stage_g.at[slot], dwg_hbm.at[span], st_sem.at[0, slot]),
            pltpu.make_async_copy(stage_u.at[slot], dwu_hbm.at[span], st_sem.at[1, slot]),
            pltpu.make_async_copy(stage_d.at[slot], dwd_hbm.at[:, span], st_sem.at[2, slot]),
        )

    tiles = width // TILE

    @pl.loop(0, tiles)
    def _(tile):
        slot = tile % 2
        span = pl.ds(pl.multiple_of(tile * TILE, TILE), TILE)

        @pl.when(tile >= 2)
        def _():
            for copy in stage_copies(tile - 2, slot):
                copy.wait()

        inputs = recv_n[:, :, :, :, :, span].reshape(2 * rows, TILE)
        stage_g[slot] = dot_tn(inputs, dgp_s[...]).astype(BF)
        stage_u[slot] = dot_tn(inputs, dup_s[...]).astype(BF)
        stage_d[slot] = dot_tn(act_s[...], recv_g[:, :, :, :, :, span].reshape(2 * rows, TILE)).astype(BF)
        for copy in stage_copies(tile, slot):
            copy.start()

    def homeward(part, par, kind):
        for g in range(GROUPS):
            me = place[g][0]
            par[g][me] = part[g][me]
        around(
            lambda g, me, to: remote(
                part[g].at[to], par[g].at[me], m_send.at[kind, g], m_recv.at[kind, g], ring_device(g, to)
            )
        )

    for g in range(GROUPS):
        await_bytes(gat_n[g].at[pl.ds(0, 3)], t_send.at[0, g])
        await_bytes(gat_g[g].at[pl.ds(0, 3)], t_send.at[1, g])
    await_half(ret_o, 2, 0)
    await_half(ret_o, 2, 1)
    for g in range(GROUPS):
        expert = jnp.broadcast_to(
            plane_expert(g, iota((PLANE, tok), 0)).astype(F32)[:, None, :], (PLANE, CAP, tok)
        ).reshape(PLANE * CAP, tok)
        for p in range(RING):
            lanes = pl.ds(p * tok, tok)
            back = ret_o[g][:, p].reshape(PLANE * CAP, wide(g))
            scores = dot_nt(back, gat_g[g][p]) * slot_s[g, 0, :, lanes].astype(F32)
            for k in range(4):
                mine = jnp.where(route[g, p, k : k + 1, :] == expert, scores, 0.0)
                gates_out[g, p, k : k + 1, :] = jnp.sum(mine, axis=0, keepdims=True)
            gat_n[g][p] = (dot_tn(slot_s[g, 1, :, lanes], back) + dot_tn(slot_s[g, 2, :, lanes], back)).astype(BF)
    for g in range(GROUPS):
        me = place[g][0]
        gates_in[g, me] = gates_out[g, me]
    homeward(gat_n, par_o, 0)
    around(
        lambda g, me, to: remote(
            gates_out.at[g, to], gates_in.at[g, me], q_send.at[1], q_recv.at[1], ring_device(g, to)
        )
    )
    exchange(ring_b, 8, dp, "dp", 1, collect(ring_a, 16, 0))

    await_half(ret_p, 3, 0)
    await_half(ret_p, 3, 1)
    for g in range(GROUPS):
        for p in range(RING):
            back = ret_p[g][:, p].reshape(PLANE * CAP, wide(g))
            gat_g[g][p] = dot_tn(slot_s[g, 0, :, pl.ds(p * tok, tok)], back).astype(BF)
    homeward(gat_g, par_p, 1)

    def four(ref):
        return (ref[0].astype(F32) + ref[1].astype(F32)) + (ref[2].astype(F32) + ref[3].astype(F32))

    for g in range(GROUPS):
        await_bytes(par_o[g].at[pl.ds(0, 3)], m_recv.at[0, g])
        moe_ref[:, cols(g)] = four(par_o[g]).astype(BF)
    await_bytes(gates_in.at[:, pl.ds(0, 3)], q_recv.at[1])
    total = jnp.zeros((4, tok), F32)
    for g in range(GROUPS):
        for p in range(RING):
            total += gates_in[g, p]
    gg_ref[...] = total
    ggain_ref[...] = collect(ring_b, 8, 1)

    for tile in range(tiles - 2, tiles):
        for copy in stage_copies(tile, tile % 2):
            copy.wait()
    for kind, shape in enumerate((send_n, send_g, ret_o, ret_p)):
        for g in range(GROUPS):
            await_bytes(shape[g].at[pl.ds(0, PLANE - 1)], s_sem.at[kind, g])
    await_bytes(route.at[:, pl.ds(0, 3)], q_send.at[0])
    await_bytes(gates_in.at[:, pl.ds(0, 3)], q_send.at[1])

    scaled_sum = jnp.zeros((tok, 1), F32)
    for g in range(GROUPS):
        await_bytes(par_p[g].at[pl.ds(0, 3)], m_recv.at[1, g])
        xhat = tokens_ref[:, cols(g)].astype(F32) * inverse_s[...]
        scaled_sum += jnp.sum(four(par_p[g]) * gain_ref[:, cols(g)] * xhat, axis=1, keepdims=True)
    mean = scaled_sum / width
    for g in range(GROUPS):
        xhat = tokens_ref[:, cols(g)].astype(F32) * inverse_s[...]
        scaled = four(par_p[g]) * gain_ref[:, cols(g)]
        tg_ref[:, cols(g)] = (inverse_s[...] * (scaled - xhat * mean)).astype(BF)
    for g in range(GROUPS):
        await_bytes(par_o[g].at[pl.ds(0, 3)], m_send.at[0, g])
        await_bytes(par_p[g].at[pl.ds(0, 3)], m_send.at[1, g])


def publish(*refs):
    count = (len(refs) - 2) // 3
    sources, targets, held = refs[:count], refs[count : 2 * count], refs[2 * count : 3 * count]
    load_sem, store_sem = refs[-2:]
    loads, stores = [], []
    for j in range(count - 1, -1, -1):
        rows = sources[j].shape[0]
        pieces = 4 if rows >= 512 else 1
        for k in range(pieces):
            part = pl.ds(k * rows // pieces, rows // pieces)
            loads.append(pltpu.make_async_copy(sources[j].at[part], held[j].at[part], load_sem.at[j, k]))
            stores.append(pltpu.make_async_copy(held[j].at[part], targets[j].at[part], store_sem.at[j, k]))
    for load in loads:
        load.start()
    for load, store in zip(loads, stores):
        load.wait()
        store.start()
    for store in stores:
        store.wait()


def body(tokens, gain, gates, expert_ids, w_gate, w_up, w_down, grad_out):
    tok, width = tokens.shape
    hidden = w_gate.shape[2]
    vmem = pl.BlockSpec(memory_space=pltpu.VMEM)
    hbm = pl.BlockSpec(memory_space=pl.ANY)
    shapes = (
        jax.ShapeDtypeStruct((tok, width), BF),
        jax.ShapeDtypeStruct((tok, width), BF),
        jax.ShapeDtypeStruct((4, tok), F32),
        jax.ShapeDtypeStruct((1, width), F32),
        jax.ShapeDtypeStruct((width, hidden), BF),
        jax.ShapeDtypeStruct((width, hidden), BF),
        jax.ShapeDtypeStruct((hidden, width), BF),
    )
    ring = [pltpu.VMEM((RING, tok, wide(g)), BF) for g in range(GROUPS)]
    plane = [pltpu.VMEM((PLANE, RING, CAP, wide(g)), BF) for g in range(GROUPS)]
    full = pltpu.VMEM((2, RING, RING, RING, CAP, width), BF)
    dma = pltpu.SemaphoreType.DMA
    outs = pl.pallas_call(
        kernel,
        name="experts",
        out_shape=shapes,
        in_specs=[vmem] * 5 + [hbm] * 3,
        out_specs=(vmem, vmem, vmem, vmem, hbm, hbm, hbm),
        scratch_shapes=ring * 2 + plane * 2 + [full] * 4 + plane * 2 + ring * 2
        + [
            pltpu.VMEM((width, hidden), BF),
            pltpu.VMEM((width, hidden), BF),
            pltpu.VMEM((hidden, width), BF),
            pltpu.VMEM((DEV * CAP, hidden), BF),
            pltpu.VMEM((DEV * CAP, hidden), BF),
            pltpu.VMEM((DEV * CAP, hidden), BF),
            pltpu.VMEM((2, TILE, hidden), BF),
            pltpu.VMEM((2, TILE, hidden), BF),
            pltpu.VMEM((2, hidden, TILE), BF),
            pltpu.VMEM((GROUPS, RING, 8, tok), F32),
            pltpu.VMEM((GROUPS, 3, PLANE * CAP, RING * tok), BF),
            pltpu.VMEM((GROUPS, RING, 4, tok), F32),
            pltpu.VMEM((GROUPS, RING, 4, tok), F32),
            pltpu.VMEM((1, width), F32),
            pltpu.VMEM((16, 1, width), F32),
            pltpu.VMEM((8, 1, width), F32),
            pltpu.VMEM((tok, 1), F32),
            dma((3,)),
            dma((4, GROUPS)),
            dma((4, 2, GROUPS)),
            dma((3, 2)),
            dma((2,)),
            dma((2,)),
            dma((2, GROUPS)),
            dma((2, GROUPS)),
            dma((2, GROUPS)),
            dma((2, GROUPS)),
            dma((2,)),
            dma((2,)),
        ],
        compiler_params=pltpu.CompilerParams(
            collective_id=0, has_side_effects=True, vmem_limit_bytes=65400 * 1024
        ),
    )(
        tokens, gain[None], expert_ids.T, gates.T, grad_out, w_gate[0], w_up[0], w_down[0],
    )
    outs = pl.pallas_call(
        publish,
        name="publish",
        out_shape=shapes,
        in_specs=[hbm] * len(shapes),
        out_specs=(hbm,) * len(shapes),
        scratch_shapes=[pltpu.VMEM(s.shape, s.dtype) for s in shapes] + [dma((len(shapes), 4))] * 2,
        compiler_params=pltpu.CompilerParams(vmem_limit_bytes=60 * 1024 * 1024),
    )(*outs)
    moe_out, token_gradient, grad_gates, gain_gradient, grad_gate, grad_up, grad_down = outs
    return (
        moe_out, token_gradient, grad_gates.T, gain_gradient[0],
        grad_gate[None], grad_up[None], grad_down[None],
    )


def solution(mesh):
    both = P(("dp", "expert"), None)
    three = P(("dp", "expert"), None, None)
    return jax.shard_map(
        body,
        mesh=mesh,
        in_specs=(both, P(), both, both, three, three, three, both),
        out_specs=(both, both, both, P(), three, three, three),
        check_vma=False,
    )
```

```python
import jax
import jax.numpy as jnp
from jax import lax
from jax.experimental import pallas as pl
from jax.experimental.pallas import tpu as pltpu
from jax.sharding import PartitionSpec as P

MESH = pl.DeviceIdType.MESH
BF = jnp.bfloat16
F32 = jnp.float32
DEV = 128
CAP = 8
RING = 4
PLANE = 32
HALF = 16
TILE = 128
CUTS = (0, 640, 1280, 2048)
GROUPS = 3
PEERS = 73


def dot(left, right):
    return jnp.dot(left, right, preferred_element_type=F32)


def dot_nt(left, right):
    return lax.dot_general(left, right, (((1,), (1,)), ((), ())), preferred_element_type=F32)


def dot_tn(left, right):
    return lax.dot_general(left, right, (((0,), (0,)), ((), ())), preferred_element_type=F32)


def iota(shape, dim):
    return lax.broadcasted_iota(jnp.int32, shape, dim)


def cols(group):
    return pl.ds(CUTS[group], CUTS[group + 1] - CUTS[group])


def wide(group):
    return CUTS[group + 1] - CUTS[group]


def device(y, c, x, z):
    return y * 2 + c, x * 4 + z


def split(group, y, x, z):
    return ((x, y, z), (y, x, z), (z, x, y))[group]


def join(group, along, first, second):
    return ((first, along, second), (along, first, second), (second, first, along))[group]


def four_of(value):
    return lax.rem(value, 4)


def plane_offsets(step):
    first = four_of(step)
    return first, four_of(first + lax.div(step, 4))


def rows_of(ref, half, group, y, x, z):
    c = cols(group)
    if group == 0:
        return ref.at[half, y, :, z, :, c]
    if group == 1:
        return ref.at[half, :, x, z, :, c]
    return ref.at[half, y, x, :, :, c]


def kernel(
    tokens_ref, gain_ref, ids_ref, gates_ref, grad_out_ref, wg_hbm, wu_hbm, wd_hbm,
    moe_ref, tg_ref, gg_ref, ggain_ref, dwg_hbm, dwu_hbm, dwd_hbm,
    gn0, gn1, gn2, gg0, gg1, gg2,
    sn0, sn1, sn2, sg0, sg1, sg2, recv_n, recv_g, out_o, out_p,
    ro0, ro1, ro2, rp0, rp1, rp2, po0, po1, po2, pp0, pp1, pp2,
    wg, wu, wd, act_s, dgp_s, dup_s, stage_g, stage_u, stage_d,
    route, slot_s, gates_out, gates_in, gain_sum, ring_a, ring_b, inverse_s,
    w_sem, s_sem, r_sem, st_sem, g_send, g_recv, t_send, t_recv, m_send, m_recv, q_send, q_recv,
):
    tok, width = tokens_ref.shape
    gat_n, gat_g = (gn0, gn1, gn2), (gg0, gg1, gg2)
    send_n, send_g = (sn0, sn1, sn2), (sg0, sg1, sg2)
    ret_o, ret_p = (ro0, ro1, ro2), (rp0, rp1, rp2)
    par_o, par_p = (po0, po1, po2), (pp0, pp1, pp2)
    dp, ex = lax.axis_index("dp"), lax.axis_index("expert")
    y, c, x, z = lax.div(dp, 2), lax.rem(dp, 2), lax.div(ex, 4), lax.rem(ex, 4)
    sign = 1 - 2 * c
    place = [split(g, y, x, z) for g in range(GROUPS)]

    barrier = pltpu.get_barrier_semaphore()

    ys, xs, zs = ([value] + [four_of(value + o) for o in (1, 2, 3)] for value in (y, x, z))
    for place_off in range(4 * 4 * 4):
        oy, ox, oz = place_off // 16, place_off // 4 % 4, place_off % 4
        if oy and ox and oz:
            continue
        for core in (c, 1 - c) if place_off else (1 - c,):
            pl.semaphore_signal(barrier, inc=1, device_id=device(ys[oy], core, xs[ox], zs[oz]), device_id_type=MESH)

    loads = [
        pltpu.make_async_copy(src, dst, w_sem.at[j])
        for j, (src, dst) in enumerate(((wg_hbm, wg), (wu_hbm, wu), (wd_hbm, wd)))
    ]
    for load in loads:
        load.start()

    own = jnp.concatenate([ids_ref[...].astype(F32), gates_ref[...]], axis=0)
    for g in range(GROUPS):
        route[g, place[g][0]] = own
        gat_g[g][place[g][0]] = grad_out_ref[:, cols(g)]

    pl.semaphore_wait(barrier, PEERS)

    def ring_device(g, along):
        yy, xx, zz = join(g, along, place[g][1], place[g][2])
        return device(yy, c, xx, zz)

    def around(start):
        for off in (1, 3, 2):
            for g in range(GROUPS):
                start(g, place[g][0], four_of(place[g][0] + off))

    def remote(src, dst, send, recv, to):
        pltpu.make_async_remote_copy(
            src_ref=src, dst_ref=dst, send_sem=send, recv_sem=recv, device_id=to, device_id_type=MESH
        ).start()

    def await_bytes(view, sem):
        pltpu.make_async_copy(view, view, sem).wait()

    around(lambda g, me, to: remote(route.at[g, me], route.at[g, me], q_send.at[0], q_recv.at[0], ring_device(g, to)))

    def gather_near(gat, kind):
        for g in range(GROUPS):
            me = place[g][0]
            for side, off in ((0, 1), (1, 3)):
                remote(
                    gat[g].at[me], gat[g].at[me], t_send.at[kind, g], t_recv.at[kind, g, side],
                    ring_device(g, four_of(me + off)),
                )

    def gather_far(gat, kind):
        for g in range(GROUPS):
            me = place[g][0]
            for side, off in ((0, 1), (1, 3)):
                await_bytes(gat[g].at[0], t_recv.at[kind, g, side])
                block = gat[g].at[four_of(me + 4 - off), pl.ds(side * (tok // 2), tok // 2)]
                remote(block, block, t_send.at[kind, g], t_recv.at[kind, g, 2], ring_device(g, four_of(me + off)))

    gather_near(gat_g, 1)
    square_sum = jnp.zeros((tok, 1), F32)
    for g in range(GROUPS):
        part = tokens_ref[:, cols(g)].astype(F32)
        square_sum += jnp.sum(part * part, axis=1, keepdims=True)
    inverse_s[...] = lax.rsqrt(square_sum / width + 1e-06)
    for g in range(GROUPS):
        xhat = tokens_ref[:, cols(g)].astype(F32) * inverse_s[...]
        gat_n[g][place[g][0]] = (xhat * gain_ref[:, cols(g)]).astype(BF)
    gather_near(gat_n, 0)
    gather_far(gat_g, 1)

    def plane_expert(g, rows):
        half, first = rows >> 4, rows & 3
        second = (first + ((rows >> 2) & 3)) & 3
        along, mine1, mine2 = place[g]
        yy, xx, zz = join(g, along, (mine1 + sign * first) & 3, (mine2 + sign * second) & 3)
        return 32 * yy + 16 * ((c + half) & 1) + 4 * xx + zz

    before = (iota((tok, tok), 0) < iota((tok, tok), 1)).astype(BF)

    def widen(rows):
        return jnp.broadcast_to(rows[:, None, :], (PLANE, CAP, tok)).reshape(PLANE * CAP, tok)

    await_bytes(route.at[:, pl.ds(0, 3)], q_recv.at[0])
    slot_rank = (iota((PLANE * CAP, tok), 0) & 7).astype(F32)
    for g in range(GROUPS):
        expert = plane_expert(g, iota((PLANE, tok), 0)).astype(F32)
        for p in range(RING):
            named = jnp.zeros((PLANE, tok), F32)
            gate = jnp.zeros((PLANE, tok), F32)
            for k in range(4):
                hit = route[g, p, k : k + 1, :] == expert
                named += hit.astype(F32)
                gate += jnp.where(hit, route[g, p, 4 + k : 5 + k, :], 0.0)
            rank = dot(named.astype(BF), before)
            live = jnp.where(widen(rank) == slot_rank, widen(named), 0.0)
            weight = live * widen(gate)
            high = weight.astype(BF)
            lanes = pl.ds(p * tok, tok)
            slot_s[g, 0, :, lanes] = live.astype(BF)
            slot_s[g, 1, :, lanes] = high
            slot_s[g, 2, :, lanes] = (weight - high.astype(F32)).astype(BF)

    def select(g, gat, send, recv, weighted, off):
        p = four_of(place[g][0] + off)
        lanes = pl.ds(pl.multiple_of(p * tok, tok), tok)
        if weighted:
            picked = dot(slot_s[g, 1, :, lanes], gat[g][p]) + dot(slot_s[g, 2, :, lanes], gat[g][p])
        else:
            picked = dot(slot_s[g, 0, :, lanes], gat[g][p])
        picked = picked.astype(BF).reshape(PLANE, CAP, wide(g))
        send[g][:, p] = picked
        if g == 0:
            recv[0, y, p, z, :, cols(g)] = picked[0]
        elif g == 1:
            recv[0, p, x, z, :, cols(g)] = picked[0]
        else:
            recv[0, y, x, p, :, cols(g)] = picked[0]

    def select_all(gat, send, recv, kind):
        for g in range(GROUPS):
            for off in (0, 1, 3):
                select(g, gat, send, recv, kind == 1, off)
        for g in range(GROUPS):
            await_bytes(gat[g].at[0], t_recv.at[kind, g, 2])
            select(g, gat, send, recv, kind == 1, 2)

    def push_out(send, recv, kind, half):
        @pl.loop(1 if half == 0 else 0, HALF)
        def _(step):
            first, second = plane_offsets(step)
            for g in range(GROUPS):
                along, mine1, mine2 = place[g]
                yy, xx, zz = join(g, along, four_of(mine1 + sign * first + 4), four_of(mine2 + sign * second + 4))
                remote(
                    send[g].at[half * HALF + step], rows_of(recv, half, g, y, x, z),
                    s_sem.at[kind, g], r_sem.at[kind, half, g], device(yy, lax.rem(c + half, 2), xx, zz),
                )

    def push_back(out, ret, kind, half):
        other = lax.rem(c + half, 2)
        turn = 1 - 2 * other

        @pl.loop(jnp.where(half == 0, 1, 0), HALF)
        def _(step):
            first, second = plane_offsets(step)
            for g in range(GROUPS):
                along, mine1, mine2 = place[g]
                yy, xx, zz = join(g, along, four_of(mine1 - turn * first + 4), four_of(mine2 - turn * second + 4))
                remote(
                    rows_of(out, half, g, yy, xx, zz), ret[g].at[half * HALF + step],
                    s_sem.at[kind, g], r_sem.at[kind, half, g], device(yy, other, xx, zz),
                )

    def await_half(shape, kind, half):
        for g in range(GROUPS):
            if isinstance(half, int):
                await_bytes(shape[g].at[pl.ds(0, HALF - 1 + half)], r_sem.at[kind, half, g])
                continue

            @pl.when(half == 0)
            def _():
                await_bytes(shape[g].at[pl.ds(0, HALF - 1)], r_sem.at[kind, 0, g])

            @pl.when(half == 1)
            def _():
                await_bytes(shape[g].at[pl.ds(0, HALF)], r_sem.at[kind, 1, g])

    gather_far(gat_n, 0)
    select_all(gat_g, send_g, recv_g, 1)
    push_out(send_g, recv_g, 1, 0)
    select_all(gat_n, send_n, recv_n, 0)
    push_out(send_n, recv_n, 0, 0)
    push_out(send_g, recv_g, 1, 1)
    push_out(send_n, recv_n, 0, 1)

    for load in loads:
        load.wait()
    gain_sum[...] = jnp.zeros_like(gain_sum)
    rows = PLANE // 2 * RING * CAP
    piece = rows // 2

    def keep(out, ret):
        for g in range(GROUPS):
            if g == 0:
                ret[g][0] = out[0, y, :, z, :, cols(g)]
            elif g == 1:
                ret[g][0] = out[0, :, x, z, :, cols(g)]
            else:
                ret[g][0] = out[0, y, x, :, :, cols(g)]

    @pl.loop(0, 4)
    def _(quarter):
        half, low = quarter // 2, quarter % 2
        span = pl.ds(pl.multiple_of(quarter * piece, piece), piece)
        lines = pl.ds(low * 2, 2)

        @pl.when(low == 0)
        def _():
            await_half(send_n, 0, half)
            await_half(send_g, 1, half)

        inputs = recv_n[half, lines].reshape(piece, width)
        gate_pre = dot(inputs, wg[...])
        up_pre = dot(inputs, wu[...])
        sig = 1.0 / (1.0 + jnp.exp(-gate_pre))
        act = (gate_pre * sig * up_pre).astype(BF)
        act_s[span, :] = act
        for j in range(0, width, 512):
            out_o[half, lines, :, :, :, j : j + 512] = (
                dot(act, wd[:, j : j + 512]).astype(BF).reshape(2, RING, RING, CAP, 512)
            )
        grad_act = dot_nt(recv_g[half, lines].reshape(piece, width), wd[...])
        dgp = (grad_act * up_pre * sig * (1.0 + gate_pre * (1.0 - sig))).astype(BF)
        dup = (grad_act * gate_pre * sig).astype(BF)
        dgp_s[span, :] = dgp
        dup_s[span, :] = dup
        for j in range(0, width, 512):
            part = (dot_nt(dgp, wg[j : j + 512, :]) + dot_nt(dup, wu[j : j + 512, :])).astype(BF)
            out_p[half, lines, :, :, :, j : j + 512] = part.reshape(2, RING, RING, CAP, 512)
            arrived = recv_n[half, lines, :, :, :, j : j + 512].reshape(piece, 512)
            gain_sum[:, j : j + 512] += jnp.sum(part.astype(F32) * arrived.astype(F32), axis=0, keepdims=True)

        @pl.when(quarter == 1)
        def _():
            keep(out_o, ret_o)
            keep(out_p, ret_p)

        @pl.when(low == 1)
        def _():
            push_back(out_o, ret_o, 2, half)
            push_back(out_p, ret_p, 3, half)

    def exchange(ring, size, index, axis, sem, value):
        ring[index] = value

        @pl.loop(1, size)
        def _(j):
            pltpu.make_async_remote_copy(
                src_ref=ring.at[index], dst_ref=ring.at[index], send_sem=g_send.at[sem], recv_sem=g_recv.at[sem],
                device_id={axis: lax.rem(index + j, size)}, device_id_type=MESH,
            ).start()

    def collect(ring, size, sem):
        view = ring.at[pl.ds(0, size - 1)]
        await_bytes(view, g_send.at[sem])
        await_bytes(view, g_recv.at[sem])
        total = ring[0]
        for j in range(1, size):
            total += ring[j]
        return total

    exchange(ring_a, 16, ex, "expert", 0, gain_sum[...] / gain_ref[...])

    def stage_copies(tile, slot):
        span = pl.ds(pl.multiple_of(tile * TILE, TILE), TILE)
        return (
            pltpu.make_async_copy(stage_g.at[slot], dwg_hbm.at[span], st_sem.at[0, slot]),
            pltpu.make_async_copy(stage_u.at[slot], dwu_hbm.at[span], st_sem.at[1, slot]),
            pltpu.make_async_copy(stage_d.at[slot], dwd_hbm.at[:, span], st_sem.at[2, slot]),
        )

    tiles = width // TILE

    @pl.loop(0, tiles)
    def _(tile):
        slot = tile % 2
        span = pl.ds(pl.multiple_of(tile * TILE, TILE), TILE)

        @pl.when(tile >= 2)
        def _():
            for copy in stage_copies(tile - 2, slot):
                copy.wait()

        inputs = recv_n[:, :, :, :, :, span].reshape(2 * rows, TILE)
        stage_g[slot] = dot_tn(inputs, dgp_s[...]).astype(BF)
        stage_u[slot] = dot_tn(inputs, dup_s[...]).astype(BF)
        stage_d[slot] = dot_tn(act_s[...], recv_g[:, :, :, :, :, span].reshape(2 * rows, TILE)).astype(BF)
        for copy in stage_copies(tile, slot):
            copy.start()

    def homeward(g, part, par, kind):
        me = place[g][0]
        for off in (2, 1, 3):
            to = four_of(me + off)
            remote(part[g].at[to], par[g].at[me], m_send.at[kind, g], m_recv.at[kind, g], ring_device(g, to))
        par[g][me] = part[g][me]

    for g in range(GROUPS):
        await_bytes(gat_n[g].at[pl.ds(0, 3)], t_send.at[0, g])
        await_bytes(gat_g[g].at[pl.ds(0, 3)], t_send.at[1, g])
    await_half(ret_o, 2, 0)
    await_half(ret_o, 2, 1)
    for g in range(GROUPS):
        expert = jnp.broadcast_to(
            plane_expert(g, iota((PLANE, tok), 0)).astype(F32)[:, None, :], (PLANE, CAP, tok)
        ).reshape(PLANE * CAP, tok)
        for p in range(RING):
            lanes = pl.ds(p * tok, tok)
            back = ret_o[g][:, p].reshape(PLANE * CAP, wide(g))
            scores = dot_nt(back, gat_g[g][p]) * slot_s[g, 0, :, lanes].astype(F32)
            for k in range(4):
                mine = jnp.where(route[g, p, k : k + 1, :] == expert, scores, 0.0)
                gates_out[g, p, k : k + 1, :] = jnp.sum(mine, axis=0, keepdims=True)
            gat_n[g][p] = (dot_tn(slot_s[g, 1, :, lanes], back) + dot_tn(slot_s[g, 2, :, lanes], back)).astype(BF)
        homeward(g, gat_n, par_o, 0)
    for g in range(GROUPS):
        me = place[g][0]
        gates_in[g, me] = gates_out[g, me]
    around(
        lambda g, me, to: remote(
            gates_out.at[g, to], gates_in.at[g, me], q_send.at[1], q_recv.at[1], ring_device(g, to)
        )
    )
    exchange(ring_b, 8, dp, "dp", 1, collect(ring_a, 16, 0))

    for g in range(GROUPS):
        await_bytes(ret_p[g].at[pl.ds(0, HALF - 1)], r_sem.at[3, 0, g])
        await_bytes(ret_p[g].at[pl.ds(0, HALF)], r_sem.at[3, 1, g])
        for p in range(RING):
            back = ret_p[g][:, p].reshape(PLANE * CAP, wide(g))
            gat_g[g][p] = dot_tn(slot_s[g, 0, :, pl.ds(p * tok, tok)], back).astype(BF)
        homeward(g, gat_g, par_p, 1)

    def four(ref):
        return (ref[0].astype(F32) + ref[1].astype(F32)) + (ref[2].astype(F32) + ref[3].astype(F32))

    for g in range(GROUPS):
        await_bytes(par_o[g].at[pl.ds(0, 3)], m_recv.at[0, g])
        moe_ref[:, cols(g)] = four(par_o[g]).astype(BF)
    await_bytes(gates_in.at[:, pl.ds(0, 3)], q_recv.at[1])
    total = jnp.zeros((4, tok), F32)
    for g in range(GROUPS):
        for p in range(RING):
            total += gates_in[g, p]
    gg_ref[...] = total
    ggain_ref[...] = collect(ring_b, 8, 1)

    for tile in range(tiles - 2, tiles):
        for copy in stage_copies(tile, tile % 2):
            copy.wait()
    for kind, shape in enumerate((send_n, send_g, ret_o, ret_p)):
        for g in range(GROUPS):
            await_bytes(shape[g].at[pl.ds(0, PLANE - 1)], s_sem.at[kind, g])
    await_bytes(route.at[:, pl.ds(0, 3)], q_send.at[0])
    await_bytes(gates_in.at[:, pl.ds(0, 3)], q_send.at[1])

    scaled_sum = jnp.zeros((tok, 1), F32)
    for g in range(GROUPS):
        await_bytes(par_p[g].at[pl.ds(0, 3)], m_recv.at[1, g])
        xhat = tokens_ref[:, cols(g)].astype(F32) * inverse_s[...]
        scaled_sum += jnp.sum(four(par_p[g]) * gain_ref[:, cols(g)] * xhat, axis=1, keepdims=True)
    mean = scaled_sum / width
    for g in range(GROUPS):
        xhat = tokens_ref[:, cols(g)].astype(F32) * inverse_s[...]
        scaled = four(par_p[g]) * gain_ref[:, cols(g)]
        tg_ref[:, cols(g)] = (inverse_s[...] * (scaled - xhat * mean)).astype(BF)
    for g in range(GROUPS):
        await_bytes(par_o[g].at[pl.ds(0, 3)], m_send.at[0, g])
        await_bytes(par_p[g].at[pl.ds(0, 3)], m_send.at[1, g])


def publish(*refs):
    count = (len(refs) - 2) // 3
    sources, targets, held = refs[:count], refs[count : 2 * count], refs[2 * count : 3 * count]
    load_sem, store_sem = refs[-2:]
    loads, stores = [], []
    for j in range(count - 1, -1, -1):
        rows = sources[j].shape[0]
        pieces = 8 if rows >= 512 else 1
        for k in range(pieces):
            part = pl.ds(k * rows // pieces, rows // pieces)
            loads.append(pltpu.make_async_copy(sources[j].at[part], held[j].at[part], load_sem.at[j, k]))
            stores.append(pltpu.make_async_copy(held[j].at[part], targets[j].at[part], store_sem.at[j, k]))
    for load in loads:
        load.start()
    for load, store in zip(loads, stores):
        load.wait()
        store.start()
    for store in stores:
        store.wait()


def body(tokens, gain, gates, expert_ids, w_gate, w_up, w_down, grad_out):
    tok, width = tokens.shape
    hidden = w_gate.shape[2]
    vmem = pl.BlockSpec(memory_space=pltpu.VMEM)
    hbm = pl.BlockSpec(memory_space=pl.ANY)
    shapes = (
        jax.ShapeDtypeStruct((tok, width), BF),
        jax.ShapeDtypeStruct((tok, width), BF),
        jax.ShapeDtypeStruct((4, tok), F32),
        jax.ShapeDtypeStruct((1, width), F32),
        jax.ShapeDtypeStruct((width, hidden), BF),
        jax.ShapeDtypeStruct((width, hidden), BF),
        jax.ShapeDtypeStruct((hidden, width), BF),
    )
    ring = [pltpu.VMEM((RING, tok, wide(g)), BF) for g in range(GROUPS)]
    plane = [pltpu.VMEM((PLANE, RING, CAP, wide(g)), BF) for g in range(GROUPS)]
    full = pltpu.VMEM((2, RING, RING, RING, CAP, width), BF)
    dma = pltpu.SemaphoreType.DMA
    outs = pl.pallas_call(
        kernel,
        name="experts",
        out_shape=shapes,
        in_specs=[vmem] * 5 + [hbm] * 3,
        out_specs=(vmem, vmem, vmem, vmem, hbm, hbm, hbm),
        scratch_shapes=ring * 2 + plane * 2 + [full] * 4 + plane * 2 + ring * 2
        + [
            pltpu.VMEM((width, hidden), BF),
            pltpu.VMEM((width, hidden), BF),
            pltpu.VMEM((hidden, width), BF),
            pltpu.VMEM((DEV * CAP, hidden), BF),
            pltpu.VMEM((DEV * CAP, hidden), BF),
            pltpu.VMEM((DEV * CAP, hidden), BF),
            pltpu.VMEM((2, TILE, hidden), BF),
            pltpu.VMEM((2, TILE, hidden), BF),
            pltpu.VMEM((2, hidden, TILE), BF),
            pltpu.VMEM((GROUPS, RING, 8, tok), F32),
            pltpu.VMEM((GROUPS, 3, PLANE * CAP, RING * tok), BF),
            pltpu.VMEM((GROUPS, RING, 4, tok), F32),
            pltpu.VMEM((GROUPS, RING, 4, tok), F32),
            pltpu.VMEM((1, width), F32),
            pltpu.VMEM((16, 1, width), F32),
            pltpu.VMEM((8, 1, width), F32),
            pltpu.VMEM((tok, 1), F32),
            dma((3,)),
            dma((4, GROUPS)),
            dma((4, 2, GROUPS)),
            dma((3, 2)),
            dma((2,)),
            dma((2,)),
            dma((2, GROUPS)),
            dma((2, GROUPS, 3)),
            dma((2, GROUPS)),
            dma((2, GROUPS)),
            dma((2,)),
            dma((2,)),
        ],
        compiler_params=pltpu.CompilerParams(
            collective_id=0, has_side_effects=True, vmem_limit_bytes=65400 * 1024
        ),
    )(
        tokens, gain[None], expert_ids.T, gates.T, grad_out, w_gate[0], w_up[0], w_down[0],
    )
    outs = pl.pallas_call(
        publish,
        name="publish",
        out_shape=shapes,
        in_specs=[hbm] * len(shapes),
        out_specs=(hbm,) * len(shapes),
        scratch_shapes=[pltpu.VMEM(s.shape, s.dtype) for s in shapes] + [dma((len(shapes), 8))] * 2,
        compiler_params=pltpu.CompilerParams(vmem_limit_bytes=60 * 1024 * 1024),
    )(*outs)
    moe_out, token_gradient, grad_gates, gain_gradient, grad_gate, grad_up, grad_down = outs
    return (
        moe_out, token_gradient, grad_gates.T, gain_gradient[0],
        grad_gate[None], grad_up[None], grad_down[None],
    )


def solution(mesh):
    both = P(("dp", "expert"), None)
    three = P(("dp", "expert"), None, None)
    return jax.shard_map(
        body,
        mesh=mesh,
        in_specs=(both, P(), both, both, three, three, three, both),
        out_specs=(both, both, both, P(), three, three, three),
        check_vma=False,
    )
```

```python
import jax
import jax.numpy as jnp
from jax import lax
from jax.experimental import pallas as pl
from jax.experimental.pallas import tpu as pltpu
from jax.sharding import PartitionSpec as P

MESH = pl.DeviceIdType.MESH
BF = jnp.bfloat16
F32 = jnp.float32
DEV = 128
CAP = 8
RING = 4
PLANE = 32
HALF = 16
TILE = 128
CUTS = (0, 640, 1280, 2048)
GROUPS = 3
PEERS = 73


def dot(left, right):
    return jnp.dot(left, right, preferred_element_type=F32)


def dot_nt(left, right):
    return lax.dot_general(left, right, (((1,), (1,)), ((), ())), preferred_element_type=F32)


def dot_tn(left, right):
    return lax.dot_general(left, right, (((0,), (0,)), ((), ())), preferred_element_type=F32)


def iota(shape, dim):
    return lax.broadcasted_iota(jnp.int32, shape, dim)


def cols(group):
    return pl.ds(CUTS[group], CUTS[group + 1] - CUTS[group])


def wide(group):
    return CUTS[group + 1] - CUTS[group]


def device(y, c, x, z):
    return y * 2 + c, x * 4 + z


def split(group, y, x, z):
    return ((x, y, z), (y, x, z), (z, x, y))[group]


def join(group, along, first, second):
    return ((first, along, second), (along, first, second), (second, first, along))[group]


def four_of(value):
    return lax.rem(value, 4)


def plane_offsets(step):
    first = four_of(step)
    return first, four_of(first + lax.div(step, 4))


def rows_of(ref, half, group, y, x, z):
    c = cols(group)
    if group == 0:
        return ref.at[half, y, :, z, :, c]
    if group == 1:
        return ref.at[half, :, x, z, :, c]
    return ref.at[half, y, x, :, :, c]


def kernel(
    tokens_hbm, gain_ref, ids_ref, gates_ref, grad_out_hbm, wg_hbm, wu_hbm, wd_hbm,
    moe_hbm, tg_hbm, gg_ref, ggain_ref, dwg_hbm, dwu_hbm, dwd_hbm,
    gn0, gn1, gn2, gg0, gg1, gg2,
    sn0, sn1, sn2, sg0, sg1, sg2, recv_n, recv_g, out_o, out_p,
    ro0, ro1, ro2, rp0, rp1, rp2, po0, po1, po2, pp0, pp1, pp2,
    wg, wu, wd, act_s, dgp_s, dup_s, stage_g, stage_u, stage_d,
    route, slot_s, gates_out, gates_in, gain_sum, ring_a, ring_b, inverse_s,
    tokens_ref, moe_ref, tg_ref,
    w_sem, s_sem, r_sem, st_sem, g_send, g_recv, t_send, t_recv, m_send, m_recv, q_send, q_recv,
    i_sem, o_sem,
):
    tok, width = tokens_ref.shape
    gat_n, gat_g = (gn0, gn1, gn2), (gg0, gg1, gg2)
    send_n, send_g = (sn0, sn1, sn2), (sg0, sg1, sg2)
    ret_o, ret_p = (ro0, ro1, ro2), (rp0, rp1, rp2)
    par_o, par_p = (po0, po1, po2), (pp0, pp1, pp2)
    dp, ex = lax.axis_index("dp"), lax.axis_index("expert")
    y, c, x, z = lax.div(dp, 2), lax.rem(dp, 2), lax.div(ex, 4), lax.rem(ex, 4)
    sign = 1 - 2 * c
    place = [split(g, y, x, z) for g in range(GROUPS)]

    barrier = pltpu.get_barrier_semaphore()

    ys, xs, zs = ([value] + [four_of(value + o) for o in (1, 2, 3)] for value in (y, x, z))
    for place_off in range(4 * 4 * 4):
        oy, ox, oz = place_off // 16, place_off // 4 % 4, place_off % 4
        if oy and ox and oz:
            continue
        for core in (c, 1 - c) if place_off else (1 - c,):
            pl.semaphore_signal(barrier, inc=1, device_id=device(ys[oy], core, xs[ox], zs[oz]), device_id_type=MESH)

    cotangents = [
        pltpu.make_async_copy(grad_out_hbm.at[:, cols(g)], gat_g[g].at[place[g][0]], i_sem.at[g]) for g in range(GROUPS)
    ]
    rows_in = pltpu.make_async_copy(tokens_hbm, tokens_ref, i_sem.at[GROUPS])
    for copy in cotangents:
        copy.start()
    rows_in.start()
    loads = [
        pltpu.make_async_copy(src, dst, w_sem.at[j])
        for j, (src, dst) in enumerate(((wg_hbm, wg), (wu_hbm, wu), (wd_hbm, wd)))
    ]
    for load in loads:
        load.start()

    own = jnp.concatenate([ids_ref[...].astype(F32), gates_ref[...]], axis=0)
    for g in range(GROUPS):
        route[g, place[g][0]] = own
        cotangents[g].wait()

    pl.semaphore_wait(barrier, PEERS)

    def ring_device(g, along):
        yy, xx, zz = join(g, along, place[g][1], place[g][2])
        return device(yy, c, xx, zz)

    def around(start):
        for off in (1, 3, 2):
            for g in range(GROUPS):
                start(g, place[g][0], four_of(place[g][0] + off))

    def remote(src, dst, send, recv, to):
        pltpu.make_async_remote_copy(
            src_ref=src, dst_ref=dst, send_sem=send, recv_sem=recv, device_id=to, device_id_type=MESH
        ).start()

    def await_bytes(view, sem):
        pltpu.make_async_copy(view, view, sem).wait()

    around(lambda g, me, to: remote(route.at[g, me], route.at[g, me], q_send.at[0], q_recv.at[0], ring_device(g, to)))

    def gather_near(gat, kind):
        for g in range(GROUPS):
            me = place[g][0]
            for side, off in ((0, 1), (1, 3)):
                remote(
                    gat[g].at[me], gat[g].at[me], t_send.at[kind, g], t_recv.at[kind, g, side],
                    ring_device(g, four_of(me + off)),
                )

    def gather_far(gat, kind):
        for g in range(GROUPS):
            me = place[g][0]
            for side, off in ((0, 1), (1, 3)):
                await_bytes(gat[g].at[0], t_recv.at[kind, g, side])
                block = gat[g].at[four_of(me + 4 - off), pl.ds(side * (tok // 2), tok // 2)]
                remote(block, block, t_send.at[kind, g], t_recv.at[kind, g, 2], ring_device(g, four_of(me + off)))

    gather_near(gat_g, 1)
    rows_in.wait()
    square_sum = jnp.zeros((tok, 1), F32)
    for g in range(GROUPS):
        part = tokens_ref[:, cols(g)].astype(F32)
        square_sum += jnp.sum(part * part, axis=1, keepdims=True)
    inverse_s[...] = lax.rsqrt(square_sum / width + 1e-06)
    for g in range(GROUPS):
        xhat = tokens_ref[:, cols(g)].astype(F32) * inverse_s[...]
        gat_n[g][place[g][0]] = (xhat * gain_ref[:, cols(g)]).astype(BF)
    gather_near(gat_n, 0)
    gather_far(gat_g, 1)

    def plane_expert(g, rows):
        half, first = rows >> 4, rows & 3
        second = (first + ((rows >> 2) & 3)) & 3
        along, mine1, mine2 = place[g]
        yy, xx, zz = join(g, along, (mine1 + sign * first) & 3, (mine2 + sign * second) & 3)
        return 32 * yy + 16 * ((c + half) & 1) + 4 * xx + zz

    before = (iota((tok, tok), 0) < iota((tok, tok), 1)).astype(BF)

    def widen(rows):
        return jnp.broadcast_to(rows[:, None, :], (PLANE, CAP, tok)).reshape(PLANE * CAP, tok)

    await_bytes(route.at[:, pl.ds(0, 3)], q_recv.at[0])
    slot_rank = (iota((PLANE * CAP, tok), 0) & 7).astype(F32)
    for g in range(GROUPS):
        expert = plane_expert(g, iota((PLANE, tok), 0)).astype(F32)
        for p in range(RING):
            named = jnp.zeros((PLANE, tok), F32)
            gate = jnp.zeros((PLANE, tok), F32)
            for k in range(4):
                hit = route[g, p, k : k + 1, :] == expert
                named += hit.astype(F32)
                gate += jnp.where(hit, route[g, p, 4 + k : 5 + k, :], 0.0)
            rank = dot(named.astype(BF), before)
            live = jnp.where(widen(rank) == slot_rank, widen(named), 0.0)
            weight = live * widen(gate)
            high = weight.astype(BF)
            lanes = pl.ds(p * tok, tok)
            slot_s[g, 0, :, lanes] = live.astype(BF)
            slot_s[g, 1, :, lanes] = high
            slot_s[g, 2, :, lanes] = (weight - high.astype(F32)).astype(BF)

    def select(g, gat, send, recv, weighted, off):
        p = four_of(place[g][0] + off)
        lanes = pl.ds(pl.multiple_of(p * tok, tok), tok)
        if weighted:
            picked = dot(slot_s[g, 1, :, lanes], gat[g][p]) + dot(slot_s[g, 2, :, lanes], gat[g][p])
        else:
            picked = dot(slot_s[g, 0, :, lanes], gat[g][p])
        picked = picked.astype(BF).reshape(PLANE, CAP, wide(g))
        send[g][:, p] = picked
        if g == 0:
            recv[0, y, p, z, :, cols(g)] = picked[0]
        elif g == 1:
            recv[0, p, x, z, :, cols(g)] = picked[0]
        else:
            recv[0, y, x, p, :, cols(g)] = picked[0]

    def select_all(gat, send, recv, kind):
        for g in range(GROUPS):
            for off in (0, 1, 3):
                select(g, gat, send, recv, kind == 1, off)
        for g in range(GROUPS):
            await_bytes(gat[g].at[0], t_recv.at[kind, g, 2])
            select(g, gat, send, recv, kind == 1, 2)

    def push_out(send, recv, kind, half):
        @pl.loop(1 if half == 0 else 0, HALF)
        def _(step):
            first, second = plane_offsets(step)
            for g in range(GROUPS):
                along, mine1, mine2 = place[g]
                yy, xx, zz = join(g, along, four_of(mine1 + sign * first + 4), four_of(mine2 + sign * second + 4))
                remote(
                    send[g].at[half * HALF + step], rows_of(recv, half, g, y, x, z),
                    s_sem.at[kind, g], r_sem.at[kind, half, g], device(yy, lax.rem(c + half, 2), xx, zz),
                )

    def push_back(out, ret, kind, half):
        other = lax.rem(c + half, 2)
        turn = 1 - 2 * other

        @pl.loop(jnp.where(half == 0, 1, 0), HALF)
        def _(step):
            first, second = plane_offsets(step)
            for g in range(GROUPS):
                along, mine1, mine2 = place[g]
                yy, xx, zz = join(g, along, four_of(mine1 - turn * first + 4), four_of(mine2 - turn * second + 4))
                remote(
                    rows_of(out, half, g, yy, xx, zz), ret[g].at[half * HALF + step],
                    s_sem.at[kind, g], r_sem.at[kind, half, g], device(yy, other, xx, zz),
                )

    def await_half(shape, kind, half):
        for g in range(GROUPS):
            if isinstance(half, int):
                await_bytes(shape[g].at[pl.ds(0, HALF - 1 + half)], r_sem.at[kind, half, g])
                continue

            @pl.when(half == 0)
            def _():
                await_bytes(shape[g].at[pl.ds(0, HALF - 1)], r_sem.at[kind, 0, g])

            @pl.when(half == 1)
            def _():
                await_bytes(shape[g].at[pl.ds(0, HALF)], r_sem.at[kind, 1, g])

    gather_far(gat_n, 0)
    select_all(gat_g, send_g, recv_g, 1)
    push_out(send_g, recv_g, 1, 0)
    select_all(gat_n, send_n, recv_n, 0)
    push_out(send_n, recv_n, 0, 0)
    push_out(send_g, recv_g, 1, 1)
    push_out(send_n, recv_n, 0, 1)

    for load in loads:
        load.wait()
    gain_sum[...] = jnp.zeros_like(gain_sum)
    rows = PLANE // 2 * RING * CAP
    piece = rows // 2

    def keep(out, ret):
        for g in range(GROUPS):
            if g == 0:
                ret[g][0] = out[0, y, :, z, :, cols(g)]
            elif g == 1:
                ret[g][0] = out[0, :, x, z, :, cols(g)]
            else:
                ret[g][0] = out[0, y, x, :, :, cols(g)]

    def exchange(ring, size, index, axis, sem, value):
        ring[index] = value

        @pl.loop(1, size)
        def _(j):
            pltpu.make_async_remote_copy(
                src_ref=ring.at[index], dst_ref=ring.at[index], send_sem=g_send.at[sem], recv_sem=g_recv.at[sem],
                device_id={axis: lax.rem(index + j, size)}, device_id_type=MESH,
            ).start()

    def collect(ring, size, sem):
        view = ring.at[pl.ds(0, size - 1)]
        await_bytes(view, g_send.at[sem])
        await_bytes(view, g_recv.at[sem])
        total = ring[0]
        for j in range(1, size):
            total += ring[j]
        return total

    @pl.loop(0, 4)
    def _(quarter):
        half, low = quarter // 2, quarter % 2
        span = pl.ds(pl.multiple_of(quarter * piece, piece), piece)
        lines = pl.ds(low * 2, 2)

        @pl.when(low == 0)
        def _():
            await_half(send_n, 0, half)
            await_half(send_g, 1, half)

        inputs = recv_n[half, lines].reshape(piece, width)
        gate_pre = dot(inputs, wg[...])
        up_pre = dot(inputs, wu[...])
        sig = 1.0 / (1.0 + jnp.exp(-gate_pre))
        act = (gate_pre * sig * up_pre).astype(BF)
        act_s[span, :] = act
        for j in range(0, width, 512):
            out_o[half, lines, :, :, :, j : j + 512] = (
                dot(act, wd[:, j : j + 512]).astype(BF).reshape(2, RING, RING, CAP, 512)
            )
        grad_act = dot_nt(recv_g[half, lines].reshape(piece, width), wd[...])
        dgp = (grad_act * up_pre * sig * (1.0 + gate_pre * (1.0 - sig))).astype(BF)
        dup = (grad_act * gate_pre * sig).astype(BF)
        dgp_s[span, :] = dgp
        dup_s[span, :] = dup
        for j in range(0, width, 512):
            part = (dot_nt(dgp, wg[j : j + 512, :]) + dot_nt(dup, wu[j : j + 512, :])).astype(BF)
            out_p[half, lines, :, :, :, j : j + 512] = part.reshape(2, RING, RING, CAP, 512)
            arrived = recv_n[half, lines, :, :, :, j : j + 512].reshape(piece, 512)
            gain_sum[:, j : j + 512] += jnp.sum(part.astype(F32) * arrived.astype(F32), axis=0, keepdims=True)

        @pl.when(quarter == 1)
        def _():
            keep(out_o, ret_o)
            keep(out_p, ret_p)

        @pl.when(quarter == 3)
        def _():
            exchange(ring_a, 16, ex, "expert", 0, gain_sum[...] / gain_ref[...])

        @pl.when(low == 1)
        def _():
            push_back(out_o, ret_o, 2, half)
            push_back(out_p, ret_p, 3, half)


    def stage_copies(tile, slot):
        span = pl.ds(pl.multiple_of(tile * TILE, TILE), TILE)
        return (
            pltpu.make_async_copy(stage_g.at[slot], dwg_hbm.at[span], st_sem.at[0, slot]),
            pltpu.make_async_copy(stage_u.at[slot], dwu_hbm.at[span], st_sem.at[1, slot]),
            pltpu.make_async_copy(stage_d.at[slot], dwd_hbm.at[:, span], st_sem.at[2, slot]),
        )

    tiles = width // TILE

    @pl.loop(0, tiles)
    def _(tile):
        slot = tile % 2
        span = pl.ds(pl.multiple_of(tile * TILE, TILE), TILE)

        @pl.when(tile >= 2)
        def _():
            for copy in stage_copies(tile - 2, slot):
                copy.wait()

        inputs = recv_n[:, :, :, :, :, span].reshape(2 * rows, TILE)
        stage_g[slot] = dot_tn(inputs, dgp_s[...]).astype(BF)
        stage_u[slot] = dot_tn(inputs, dup_s[...]).astype(BF)
        stage_d[slot] = dot_tn(act_s[...], recv_g[:, :, :, :, :, span].reshape(2 * rows, TILE)).astype(BF)
        for copy in stage_copies(tile, slot):
            copy.start()

    def homeward(g, part, par, kind):
        me = place[g][0]
        for off in (2, 1, 3):
            to = four_of(me + off)
            remote(part[g].at[to], par[g].at[me], m_send.at[kind, g], m_recv.at[kind, g], ring_device(g, to))
        par[g][me] = part[g][me]

    exchange(ring_b, 8, dp, "dp", 1, collect(ring_a, 16, 0))
    for g in range(GROUPS):
        await_bytes(gat_n[g].at[pl.ds(0, 3)], t_send.at[0, g])
        await_bytes(gat_g[g].at[pl.ds(0, 3)], t_send.at[1, g])
    await_half(ret_o, 2, 0)
    await_half(ret_o, 2, 1)
    for g in range(GROUPS):
        expert = jnp.broadcast_to(
            plane_expert(g, iota((PLANE, tok), 0)).astype(F32)[:, None, :], (PLANE, CAP, tok)
        ).reshape(PLANE * CAP, tok)
        for p in range(RING):
            lanes = pl.ds(p * tok, tok)
            back = ret_o[g][:, p].reshape(PLANE * CAP, wide(g))
            scores = dot_nt(back, gat_g[g][p]) * slot_s[g, 0, :, lanes].astype(F32)
            for k in range(4):
                mine = jnp.where(route[g, p, k : k + 1, :] == expert, scores, 0.0)
                gates_out[g, p, k : k + 1, :] = jnp.sum(mine, axis=0, keepdims=True)
            gat_n[g][p] = (dot_tn(slot_s[g, 1, :, lanes], back) + dot_tn(slot_s[g, 2, :, lanes], back)).astype(BF)
        homeward(g, gat_n, par_o, 0)
    for g in range(GROUPS):
        me = place[g][0]
        gates_in[g, me] = gates_out[g, me]
    around(
        lambda g, me, to: remote(
            gates_out.at[g, to], gates_in.at[g, me], q_send.at[1], q_recv.at[1], ring_device(g, to)
        )
    )

    for g in range(GROUPS):
        await_bytes(ret_p[g].at[pl.ds(0, HALF - 1)], r_sem.at[3, 0, g])
        await_bytes(ret_p[g].at[pl.ds(0, HALF)], r_sem.at[3, 1, g])
        for p in range(RING):
            back = ret_p[g][:, p].reshape(PLANE * CAP, wide(g))
            gat_g[g][p] = dot_tn(slot_s[g, 0, :, pl.ds(p * tok, tok)], back).astype(BF)
        homeward(g, gat_g, par_p, 1)

    def four(ref):
        return (ref[0].astype(F32) + ref[1].astype(F32)) + (ref[2].astype(F32) + ref[3].astype(F32))

    for g in range(GROUPS):
        await_bytes(par_o[g].at[pl.ds(0, 3)], m_recv.at[0, g])
        moe_ref[:, cols(g)] = four(par_o[g]).astype(BF)
    moe_copy = pltpu.make_async_copy(moe_ref, moe_hbm, o_sem.at[GROUPS])
    moe_copy.start()
    await_bytes(gates_in.at[:, pl.ds(0, 3)], q_recv.at[1])
    total = jnp.zeros((4, tok), F32)
    for g in range(GROUPS):
        for p in range(RING):
            total += gates_in[g, p]
    gg_ref[...] = total
    ggain_ref[...] = collect(ring_b, 8, 1)

    for tile in range(tiles - 2, tiles):
        for copy in stage_copies(tile, tile % 2):
            copy.wait()
    for kind, shape in enumerate((send_n, send_g, ret_o, ret_p)):
        for g in range(GROUPS):
            await_bytes(shape[g].at[pl.ds(0, PLANE - 1)], s_sem.at[kind, g])
    await_bytes(route.at[:, pl.ds(0, 3)], q_send.at[0])
    await_bytes(gates_in.at[:, pl.ds(0, 3)], q_send.at[1])

    scaled_sum = jnp.zeros((tok, 1), F32)
    for g in range(GROUPS):
        await_bytes(par_p[g].at[pl.ds(0, 3)], m_recv.at[1, g])
        xhat = tokens_ref[:, cols(g)].astype(F32) * inverse_s[...]
        scaled_sum += jnp.sum(four(par_p[g]) * gain_ref[:, cols(g)] * xhat, axis=1, keepdims=True)
    mean = scaled_sum / width
    for g in range(GROUPS):
        xhat = tokens_ref[:, cols(g)].astype(F32) * inverse_s[...]
        scaled = four(par_p[g]) * gain_ref[:, cols(g)]
        tg_ref[:, cols(g)] = (inverse_s[...] * (scaled - xhat * mean)).astype(BF)
        pltpu.make_async_copy(tg_ref.at[:, cols(g)], tg_hbm.at[:, cols(g)], o_sem.at[g]).start()
    moe_copy.wait()
    for g in range(GROUPS):
        await_bytes(par_o[g].at[pl.ds(0, 3)], m_send.at[0, g])
        await_bytes(par_p[g].at[pl.ds(0, 3)], m_send.at[1, g])
        pltpu.make_async_copy(tg_ref.at[:, cols(g)], tg_hbm.at[:, cols(g)], o_sem.at[g]).wait()


def publish(*refs):
    count = (len(refs) - 2) // 3
    sources, targets, held = refs[:count], refs[count : 2 * count], refs[2 * count : 3 * count]
    load_sem, store_sem = refs[-2:]
    loads, stores = [], []
    for j in range(count - 1, -1, -1):
        rows = sources[j].shape[0]
        pieces = 4 if rows >= 512 else 1
        for k in range(pieces):
            part = pl.ds(k * rows // pieces, rows // pieces)
            loads.append(pltpu.make_async_copy(sources[j].at[part], held[j].at[part], load_sem.at[j, k]))
            stores.append(pltpu.make_async_copy(held[j].at[part], targets[j].at[part], store_sem.at[j, k]))
    for load in loads:
        load.start()
    for load, store in zip(loads, stores):
        load.wait()
        store.start()
    for store in stores:
        store.wait()


def body(tokens, gain, gates, expert_ids, w_gate, w_up, w_down, grad_out):
    tok, width = tokens.shape
    hidden = w_gate.shape[2]
    vmem = pl.BlockSpec(memory_space=pltpu.VMEM)
    hbm = pl.BlockSpec(memory_space=pl.ANY)
    shapes = (
        jax.ShapeDtypeStruct((tok, width), BF),
        jax.ShapeDtypeStruct((tok, width), BF),
        jax.ShapeDtypeStruct((4, tok), F32),
        jax.ShapeDtypeStruct((1, width), F32),
        jax.ShapeDtypeStruct((width, hidden), BF),
        jax.ShapeDtypeStruct((width, hidden), BF),
        jax.ShapeDtypeStruct((hidden, width), BF),
    )
    ring = [pltpu.VMEM((RING, tok, wide(g)), BF) for g in range(GROUPS)]
    plane = [pltpu.VMEM((PLANE, RING, CAP, wide(g)), BF) for g in range(GROUPS)]
    full = pltpu.VMEM((2, RING, RING, RING, CAP, width), BF)
    dma = pltpu.SemaphoreType.DMA
    outs = pl.pallas_call(
        kernel,
        name="experts",
        out_shape=shapes,
        in_specs=[hbm, vmem, vmem, vmem] + [hbm] * 4,
        out_specs=(hbm, hbm, vmem, vmem, hbm, hbm, hbm),
        scratch_shapes=ring * 2 + plane * 2 + [full] * 4 + plane * 2 + ring * 2
        + [
            pltpu.VMEM((width, hidden), BF),
            pltpu.VMEM((width, hidden), BF),
            pltpu.VMEM((hidden, width), BF),
            pltpu.VMEM((DEV * CAP, hidden), BF),
            pltpu.VMEM((DEV * CAP, hidden), BF),
            pltpu.VMEM((DEV * CAP, hidden), BF),
            pltpu.VMEM((2, TILE, hidden), BF),
            pltpu.VMEM((2, TILE, hidden), BF),
            pltpu.VMEM((2, hidden, TILE), BF),
            pltpu.VMEM((GROUPS, RING, 8, tok), F32),
            pltpu.VMEM((GROUPS, 3, PLANE * CAP, RING * tok), BF),
            pltpu.VMEM((GROUPS, RING, 4, tok), F32),
            pltpu.VMEM((GROUPS, RING, 4, tok), F32),
            pltpu.VMEM((1, width), F32),
            pltpu.VMEM((16, 1, width), F32),
            pltpu.VMEM((8, 1, width), F32),
            pltpu.VMEM((tok, 1), F32),
        ]
        + [pltpu.VMEM((tok, width), BF)] * 3
        + [
            dma((3,)),
            dma((4, GROUPS)),
            dma((4, 2, GROUPS)),
            dma((3, 2)),
            dma((2,)),
            dma((2,)),
            dma((2, GROUPS)),
            dma((2, GROUPS, 3)),
            dma((2, GROUPS)),
            dma((2, GROUPS)),
            dma((2,)),
            dma((2,)),
            dma((GROUPS + 1,)),
            dma((GROUPS + 1,)),
        ],
        compiler_params=pltpu.CompilerParams(
            collective_id=0, has_side_effects=True, vmem_limit_bytes=65400 * 1024
        ),
    )(
        tokens, gain[None], expert_ids.T, gates.T, grad_out, w_gate[0], w_up[0], w_down[0],
    )
    outs = pl.pallas_call(
        publish,
        name="publish",
        out_shape=shapes,
        in_specs=[hbm] * len(shapes),
        out_specs=(hbm,) * len(shapes),
        scratch_shapes=[pltpu.VMEM(s.shape, s.dtype) for s in shapes] + [dma((len(shapes), 4))] * 2,
        compiler_params=pltpu.CompilerParams(vmem_limit_bytes=60 * 1024 * 1024),
    )(*outs)
    moe_out, token_gradient, grad_gates, gain_gradient, grad_gate, grad_up, grad_down = outs
    return (
        moe_out, token_gradient, grad_gates.T, gain_gradient[0],
        grad_gate[None], grad_up[None], grad_down[None],
    )


def solution(mesh):
    both = P(("dp", "expert"), None)
    three = P(("dp", "expert"), None, None)
    return jax.shard_map(
        body,
        mesh=mesh,
        in_specs=(both, P(), both, both, three, three, three, both),
        out_specs=(both, both, both, P(), three, three, three),
        check_vma=False,
    )
```

```python
import jax
import jax.numpy as jnp
from jax import lax
from jax.experimental import pallas as pl
from jax.experimental.pallas import tpu as pltpu
from jax.sharding import PartitionSpec as P

MESH = pl.DeviceIdType.MESH
BF = jnp.bfloat16
F32 = jnp.float32
DEV = 128
CAP = 8
RING = 4
PLANE = 32
HALF = 16
TILE = 128
CUTS = (0, 640, 1280, 2048)
GROUPS = 3
PEERS = 73


def dot(left, right):
    return jnp.dot(left, right, preferred_element_type=F32)


def dot_nt(left, right):
    return lax.dot_general(left, right, (((1,), (1,)), ((), ())), preferred_element_type=F32)


def dot_tn(left, right):
    return lax.dot_general(left, right, (((0,), (0,)), ((), ())), preferred_element_type=F32)


def iota(shape, dim):
    return lax.broadcasted_iota(jnp.int32, shape, dim)


def cols(group):
    return pl.ds(CUTS[group], CUTS[group + 1] - CUTS[group])


def wide(group):
    return CUTS[group + 1] - CUTS[group]


def device(y, c, x, z):
    return y * 2 + c, x * 4 + z


def split(group, y, x, z):
    return ((x, y, z), (y, x, z), (z, x, y))[group]


def join(group, along, first, second):
    return ((first, along, second), (along, first, second), (second, first, along))[group]


def four_of(value):
    return lax.rem(value, 4)


def plane_offsets(step):
    first = four_of(step)
    return first, four_of(first + lax.div(step, 4))


def rows_of(ref, half, group, y, x, z):
    c = cols(group)
    if group == 0:
        return ref.at[half, y, :, z, :, c]
    if group == 1:
        return ref.at[half, :, x, z, :, c]
    return ref.at[half, y, x, :, :, c]


def kernel(
    tokens_hbm, gain_ref, ids_ref, gates_ref, grad_out_hbm, wg_hbm, wu_hbm, wd_hbm,
    moe_hbm, tg_hbm, gg_ref, ggain_ref, dwg_hbm, dwu_hbm, dwd_hbm,
    gn0, gn1, gn2, gg0, gg1, gg2,
    sn0, sn1, sn2, sg0, sg1, sg2, recv_n, recv_g, out_o, out_p,
    ro0, ro1, ro2, rp0, rp1, rp2, po0, po1, po2, pp0, pp1, pp2,
    wg, wu, wd, act_s, dgp_s, dup_s, stage_g, stage_u, stage_d,
    route, slot_s, gates_out, gates_in, gain_sum, ring_a, ring_b, inverse_s,
    tokens_ref, moe_ref, tg_ref,
    w_sem, s_sem, r_sem, st_sem, g_send, g_recv, t_send, t_recv, m_send, m_recv, q_send, q_recv,
    i_sem, o_sem,
):
    tok, width = tokens_ref.shape
    gat_n, gat_g = (gn0, gn1, gn2), (gg0, gg1, gg2)
    send_n, send_g = (sn0, sn1, sn2), (sg0, sg1, sg2)
    ret_o, ret_p = (ro0, ro1, ro2), (rp0, rp1, rp2)
    par_o, par_p = (po0, po1, po2), (pp0, pp1, pp2)
    dp, ex = lax.axis_index("dp"), lax.axis_index("expert")
    y, c, x, z = lax.div(dp, 2), lax.rem(dp, 2), lax.div(ex, 4), lax.rem(ex, 4)
    sign = 1 - 2 * c
    place = [split(g, y, x, z) for g in range(GROUPS)]

    barrier = pltpu.get_barrier_semaphore()

    ys, xs, zs = ([value] + [four_of(value + o) for o in (1, 2, 3)] for value in (y, x, z))
    for place_off in range(4 * 4 * 4):
        oy, ox, oz = place_off // 16, place_off // 4 % 4, place_off % 4
        if oy and ox and oz:
            continue
        for core in (c, 1 - c) if place_off else (1 - c,):
            pl.semaphore_signal(barrier, inc=1, device_id=device(ys[oy], core, xs[ox], zs[oz]), device_id_type=MESH)

    cotangents = [
        pltpu.make_async_copy(grad_out_hbm.at[:, cols(g)], gat_g[g].at[place[g][0]], i_sem.at[g]) for g in range(GROUPS)
    ]
    rows_in = pltpu.make_async_copy(tokens_hbm, tokens_ref, i_sem.at[GROUPS])
    for copy in cotangents:
        copy.start()
    rows_in.start()
    loads = [
        pltpu.make_async_copy(src, dst, w_sem.at[j])
        for j, (src, dst) in enumerate(((wg_hbm, wg), (wu_hbm, wu), (wd_hbm, wd)))
    ]
    for load in loads:
        load.start()

    own = jnp.concatenate([ids_ref[...].astype(F32), gates_ref[...]], axis=0)
    for g in range(GROUPS):
        route[g, place[g][0]] = own
        cotangents[g].wait()

    pl.semaphore_wait(barrier, PEERS)

    def ring_device(g, along):
        yy, xx, zz = join(g, along, place[g][1], place[g][2])
        return device(yy, c, xx, zz)

    def around(start):
        for off in (1, 3, 2):
            for g in range(GROUPS):
                start(g, place[g][0], four_of(place[g][0] + off))

    def remote(src, dst, send, recv, to):
        pltpu.make_async_remote_copy(
            src_ref=src, dst_ref=dst, send_sem=send, recv_sem=recv, device_id=to, device_id_type=MESH
        ).start()

    def await_bytes(view, sem):
        pltpu.make_async_copy(view, view, sem).wait()

    around(lambda g, me, to: remote(route.at[g, me], route.at[g, me], q_send.at[0], q_recv.at[0], ring_device(g, to)))

    def gather_near(gat, kind):
        for g in range(GROUPS):
            me = place[g][0]
            for side, off in ((0, 1), (1, 3)):
                remote(
                    gat[g].at[me], gat[g].at[me], t_send.at[kind, g], t_recv.at[kind, g, side],
                    ring_device(g, four_of(me + off)),
                )

    def gather_far(gat, kind):
        for g in range(GROUPS):
            me = place[g][0]
            for side, off in ((0, 1), (1, 3)):
                await_bytes(gat[g].at[0], t_recv.at[kind, g, side])
                block = gat[g].at[four_of(me + 4 - off), pl.ds(side * (tok // 2), tok // 2)]
                remote(block, block, t_send.at[kind, g], t_recv.at[kind, g, 2], ring_device(g, four_of(me + off)))

    gather_near(gat_g, 1)
    rows_in.wait()
    square_sum = jnp.zeros((tok, 1), F32)
    for g in range(GROUPS):
        part = tokens_ref[:, cols(g)].astype(F32)
        square_sum += jnp.sum(part * part, axis=1, keepdims=True)
    inverse_s[...] = lax.rsqrt(square_sum / width + 1e-06)
    for g in range(GROUPS):
        xhat = tokens_ref[:, cols(g)].astype(F32) * inverse_s[...]
        gat_n[g][place[g][0]] = (xhat * gain_ref[:, cols(g)]).astype(BF)
    gather_near(gat_n, 0)
    gather_far(gat_g, 1)

    def plane_expert(g, rows):
        half, first = rows >> 4, rows & 3
        second = (first + ((rows >> 2) & 3)) & 3
        along, mine1, mine2 = place[g]
        yy, xx, zz = join(g, along, (mine1 + sign * first) & 3, (mine2 + sign * second) & 3)
        return 32 * yy + 16 * ((c + half) & 1) + 4 * xx + zz

    before = (iota((tok, tok), 0) < iota((tok, tok), 1)).astype(BF)

    def widen(rows):
        return jnp.broadcast_to(rows[:, None, :], (PLANE, CAP, tok)).reshape(PLANE * CAP, tok)

    await_bytes(route.at[:, pl.ds(0, 3)], q_recv.at[0])
    slot_rank = (iota((PLANE * CAP, tok), 0) & 7).astype(F32)
    for g in range(GROUPS):
        expert = plane_expert(g, iota((PLANE, tok), 0)).astype(F32)
        for p in range(RING):
            named = jnp.zeros((PLANE, tok), F32)
            gate = jnp.zeros((PLANE, tok), F32)
            for k in range(4):
                hit = route[g, p, k : k + 1, :] == expert
                named += hit.astype(F32)
                gate += jnp.where(hit, route[g, p, 4 + k : 5 + k, :], 0.0)
            rank = dot(named.astype(BF), before)
            live = jnp.where(widen(rank) == slot_rank, widen(named), 0.0)
            weight = live * widen(gate)
            high = weight.astype(BF)
            lanes = pl.ds(p * tok, tok)
            slot_s[g, 0, :, lanes] = live.astype(BF)
            slot_s[g, 1, :, lanes] = high
            slot_s[g, 2, :, lanes] = (weight - high.astype(F32)).astype(BF)

    def select(g, gat, send, recv, weighted, off):
        p = four_of(place[g][0] + off)
        lanes = pl.ds(pl.multiple_of(p * tok, tok), tok)
        if weighted:
            picked = dot(slot_s[g, 1, :, lanes], gat[g][p]) + dot(slot_s[g, 2, :, lanes], gat[g][p])
        else:
            picked = dot(slot_s[g, 0, :, lanes], gat[g][p])
        picked = picked.astype(BF).reshape(PLANE, CAP, wide(g))
        send[g][:, p] = picked
        if g == 0:
            recv[0, y, p, z, :, cols(g)] = picked[0]
        elif g == 1:
            recv[0, p, x, z, :, cols(g)] = picked[0]
        else:
            recv[0, y, x, p, :, cols(g)] = picked[0]

    def select_all(gat, send, recv, kind):
        for g in range(GROUPS):
            for off in (0, 1, 3):
                select(g, gat, send, recv, kind == 1, off)
        for g in range(GROUPS):
            await_bytes(gat[g].at[0], t_recv.at[kind, g, 2])
            select(g, gat, send, recv, kind == 1, 2)

    def push_out(send, recv, kind, half):
        @pl.loop(1 if half == 0 else 0, HALF)
        def _(step):
            first, second = plane_offsets(step)
            for g in range(GROUPS):
                along, mine1, mine2 = place[g]
                yy, xx, zz = join(g, along, four_of(mine1 + sign * first + 4), four_of(mine2 + sign * second + 4))
                remote(
                    send[g].at[half * HALF + step], rows_of(recv, half, g, y, x, z),
                    s_sem.at[kind, g], r_sem.at[kind, half, g], device(yy, lax.rem(c + half, 2), xx, zz),
                )

    def push_back(out, ret, kind, half):
        other = lax.rem(c + half, 2)
        turn = 1 - 2 * other

        @pl.loop(jnp.where(half == 0, 1, 0), HALF)
        def _(step):
            first, second = plane_offsets(step)
            for g in range(GROUPS):
                along, mine1, mine2 = place[g]
                yy, xx, zz = join(g, along, four_of(mine1 - turn * first + 4), four_of(mine2 - turn * second + 4))
                remote(
                    rows_of(out, half, g, yy, xx, zz), ret[g].at[half * HALF + step],
                    s_sem.at[kind, g], r_sem.at[kind, half, g], device(yy, other, xx, zz),
                )

    def await_half(shape, kind, half):
        for g in range(GROUPS):
            if isinstance(half, int):
                await_bytes(shape[g].at[pl.ds(0, HALF - 1 + half)], r_sem.at[kind, half, g])
                continue

            @pl.when(half == 0)
            def _():
                await_bytes(shape[g].at[pl.ds(0, HALF - 1)], r_sem.at[kind, 0, g])

            @pl.when(half == 1)
            def _():
                await_bytes(shape[g].at[pl.ds(0, HALF)], r_sem.at[kind, 1, g])

    gather_far(gat_n, 0)
    select_all(gat_g, send_g, recv_g, 1)
    push_out(send_g, recv_g, 1, 0)
    select_all(gat_n, send_n, recv_n, 0)
    push_out(send_n, recv_n, 0, 0)
    push_out(send_g, recv_g, 1, 1)
    push_out(send_n, recv_n, 0, 1)

    for load in loads:
        load.wait()
    gain_sum[...] = jnp.zeros_like(gain_sum)
    rows = PLANE // 2 * RING * CAP
    piece = rows // 2

    def keep(out, ret):
        for g in range(GROUPS):
            if g == 0:
                ret[g][0] = out[0, y, :, z, :, cols(g)]
            elif g == 1:
                ret[g][0] = out[0, :, x, z, :, cols(g)]
            else:
                ret[g][0] = out[0, y, x, :, :, cols(g)]

    def exchange(ring, size, index, axis, sem, value):
        ring[index] = value

        @pl.loop(1, size)
        def _(j):
            pltpu.make_async_remote_copy(
                src_ref=ring.at[index], dst_ref=ring.at[index], send_sem=g_send.at[sem], recv_sem=g_recv.at[sem],
                device_id={axis: lax.rem(index + j, size)}, device_id_type=MESH,
            ).start()

    def collect(ring, size, sem):
        view = ring.at[pl.ds(0, size - 1)]
        await_bytes(view, g_send.at[sem])
        await_bytes(view, g_recv.at[sem])
        total = ring[0]
        for j in range(1, size):
            total += ring[j]
        return total

    @pl.loop(0, 4)
    def _(quarter):
        half, low = quarter // 2, quarter % 2
        span = pl.ds(pl.multiple_of(quarter * piece, piece), piece)
        lines = pl.ds(low * 2, 2)

        @pl.when(low == 0)
        def _():
            await_half(send_n, 0, half)
            await_half(send_g, 1, half)

        inputs = recv_n[half, lines].reshape(piece, width)
        gate_pre = dot(inputs, wg[...])
        up_pre = dot(inputs, wu[...])
        sig = 1.0 / (1.0 + jnp.exp(-gate_pre))
        act = (gate_pre * sig * up_pre).astype(BF)
        act_s[span, :] = act
        for j in range(0, width, 512):
            out_o[half, lines, :, :, :, j : j + 512] = (
                dot(act, wd[:, j : j + 512]).astype(BF).reshape(2, RING, RING, CAP, 512)
            )
        grad_act = dot_nt(recv_g[half, lines].reshape(piece, width), wd[...])
        dgp = (grad_act * up_pre * sig * (1.0 + gate_pre * (1.0 - sig))).astype(BF)
        dup = (grad_act * gate_pre * sig).astype(BF)
        dgp_s[span, :] = dgp
        dup_s[span, :] = dup
        for j in range(0, width, 512):
            part = (dot_nt(dgp, wg[j : j + 512, :]) + dot_nt(dup, wu[j : j + 512, :])).astype(BF)
            out_p[half, lines, :, :, :, j : j + 512] = part.reshape(2, RING, RING, CAP, 512)
            arrived = recv_n[half, lines, :, :, :, j : j + 512].reshape(piece, 512)
            gain_sum[:, j : j + 512] += jnp.sum(part.astype(F32) * arrived.astype(F32), axis=0, keepdims=True)

        @pl.when(quarter == 1)
        def _():
            keep(out_o, ret_o)
            keep(out_p, ret_p)

        @pl.when(quarter == 3)
        def _():
            exchange(ring_a, 16, ex, "expert", 0, gain_sum[...] / gain_ref[...])

        @pl.when(low == 1)
        def _():
            push_back(out_o, ret_o, 2, half)
            push_back(out_p, ret_p, 3, half)


    def stage_copies(tile, slot):
        span = pl.ds(pl.multiple_of(tile * TILE, TILE), TILE)
        return (
            pltpu.make_async_copy(stage_g.at[slot], dwg_hbm.at[span], st_sem.at[0, slot]),
            pltpu.make_async_copy(stage_u.at[slot], dwu_hbm.at[span], st_sem.at[1, slot]),
            pltpu.make_async_copy(stage_d.at[slot], dwd_hbm.at[:, span], st_sem.at[2, slot]),
        )

    tiles = width // TILE

    @pl.loop(0, tiles)
    def _(tile):
        slot = tile % 2
        span = pl.ds(pl.multiple_of(tile * TILE, TILE), TILE)

        @pl.when(tile >= 2)
        def _():
            for copy in stage_copies(tile - 2, slot):
                copy.wait()

        inputs = recv_n[:, :, :, :, :, span].reshape(2 * rows, TILE)
        stage_g[slot] = dot_tn(inputs, dgp_s[...]).astype(BF)
        stage_u[slot] = dot_tn(inputs, dup_s[...]).astype(BF)
        stage_d[slot] = dot_tn(act_s[...], recv_g[:, :, :, :, :, span].reshape(2 * rows, TILE)).astype(BF)
        for copy in stage_copies(tile, slot):
            copy.start()

    def homeward(g, part, par, kind):
        me = place[g][0]
        for off in (2, 1, 3):
            to = four_of(me + off)
            remote(part[g].at[to], par[g].at[me], m_send.at[kind, g], m_recv.at[kind, g], ring_device(g, to))
        par[g][me] = part[g][me]

    exchange(ring_b, 8, dp, "dp", 1, collect(ring_a, 16, 0))
    for g in range(GROUPS):
        await_bytes(gat_n[g].at[pl.ds(0, 3)], t_send.at[0, g])
        await_bytes(gat_g[g].at[pl.ds(0, 3)], t_send.at[1, g])
    await_half(ret_o, 2, 0)
    await_half(ret_o, 2, 1)
    for g in range(GROUPS):
        expert = jnp.broadcast_to(
            plane_expert(g, iota((PLANE, tok), 0)).astype(F32)[:, None, :], (PLANE, CAP, tok)
        ).reshape(PLANE * CAP, tok)
        for p in range(RING):
            lanes = pl.ds(p * tok, tok)
            back = ret_o[g][:, p].reshape(PLANE * CAP, wide(g))
            scores = dot_nt(back, gat_g[g][p]) * slot_s[g, 0, :, lanes].astype(F32)
            for k in range(4):
                mine = jnp.where(route[g, p, k : k + 1, :] == expert, scores, 0.0)
                gates_out[g, p, k : k + 1, :] = jnp.sum(mine, axis=0, keepdims=True)
            gat_n[g][p] = (dot_tn(slot_s[g, 1, :, lanes], back) + dot_tn(slot_s[g, 2, :, lanes], back)).astype(BF)
        homeward(g, gat_n, par_o, 0)
    for g in range(GROUPS):
        me = place[g][0]
        gates_in[g, me] = gates_out[g, me]
    around(
        lambda g, me, to: remote(
            gates_out.at[g, to], gates_in.at[g, me], q_send.at[1], q_recv.at[1], ring_device(g, to)
        )
    )

    for g in range(GROUPS):
        await_bytes(ret_p[g].at[pl.ds(0, HALF - 1)], r_sem.at[3, 0, g])
        await_bytes(ret_p[g].at[pl.ds(0, HALF)], r_sem.at[3, 1, g])
        for p in range(RING):
            back = ret_p[g][:, p].reshape(PLANE * CAP, wide(g))
            gat_g[g][p] = dot_tn(slot_s[g, 0, :, pl.ds(p * tok, tok)], back).astype(BF)
        homeward(g, gat_g, par_p, 1)

    def four(ref):
        return (ref[0].astype(F32) + ref[1].astype(F32)) + (ref[2].astype(F32) + ref[3].astype(F32))

    for g in range(GROUPS):
        await_bytes(par_o[g].at[pl.ds(0, 3)], m_recv.at[0, g])
        moe_ref[:, cols(g)] = four(par_o[g]).astype(BF)
    moe_copy = pltpu.make_async_copy(moe_ref, moe_hbm, o_sem.at[GROUPS])
    moe_copy.start()
    await_bytes(gates_in.at[:, pl.ds(0, 3)], q_recv.at[1])
    total = jnp.zeros((4, tok), F32)
    for g in range(GROUPS):
        for p in range(RING):
            total += gates_in[g, p]
    gg_ref[...] = total
    ggain_ref[...] = collect(ring_b, 8, 1)

    for tile in range(tiles - 2, tiles):
        for copy in stage_copies(tile, tile % 2):
            copy.wait()
    for kind, shape in enumerate((send_n, send_g, ret_o, ret_p)):
        for g in range(GROUPS):
            await_bytes(shape[g].at[pl.ds(0, PLANE - 1)], s_sem.at[kind, g])
    await_bytes(route.at[:, pl.ds(0, 3)], q_send.at[0])
    await_bytes(gates_in.at[:, pl.ds(0, 3)], q_send.at[1])

    scaled_sum = jnp.zeros((tok, 1), F32)
    for g in range(GROUPS):
        await_bytes(par_p[g].at[pl.ds(0, 3)], m_recv.at[1, g])
        xhat = tokens_ref[:, cols(g)].astype(F32) * inverse_s[...]
        scaled_sum += jnp.sum(four(par_p[g]) * gain_ref[:, cols(g)] * xhat, axis=1, keepdims=True)
    mean = scaled_sum / width
    for g in range(GROUPS):
        xhat = tokens_ref[:, cols(g)].astype(F32) * inverse_s[...]
        scaled = four(par_p[g]) * gain_ref[:, cols(g)]
        tg_ref[:, cols(g)] = (inverse_s[...] * (scaled - xhat * mean)).astype(BF)
        pltpu.make_async_copy(tg_ref.at[:, cols(g)], tg_hbm.at[:, cols(g)], o_sem.at[g]).start()
    moe_copy.wait()
    for g in range(GROUPS):
        await_bytes(par_o[g].at[pl.ds(0, 3)], m_send.at[0, g])
        await_bytes(par_p[g].at[pl.ds(0, 3)], m_send.at[1, g])
        pltpu.make_async_copy(tg_ref.at[:, cols(g)], tg_hbm.at[:, cols(g)], o_sem.at[g]).wait()


def publish(*refs):
    count = len(refs) // 2
    for src, dst in zip(refs[:count], refs[count:]):
        dst[...] = src[...]


def body(tokens, gain, gates, expert_ids, w_gate, w_up, w_down, grad_out):
    tok, width = tokens.shape
    hidden = w_gate.shape[2]
    vmem = pl.BlockSpec(memory_space=pltpu.VMEM)
    hbm = pl.BlockSpec(memory_space=pl.ANY)
    shapes = (
        jax.ShapeDtypeStruct((tok, width), BF),
        jax.ShapeDtypeStruct((tok, width), BF),
        jax.ShapeDtypeStruct((4, tok), F32),
        jax.ShapeDtypeStruct((1, width), F32),
        jax.ShapeDtypeStruct((width, hidden), BF),
        jax.ShapeDtypeStruct((width, hidden), BF),
        jax.ShapeDtypeStruct((hidden, width), BF),
    )
    ring = [pltpu.VMEM((RING, tok, wide(g)), BF) for g in range(GROUPS)]
    plane = [pltpu.VMEM((PLANE, RING, CAP, wide(g)), BF) for g in range(GROUPS)]
    full = pltpu.VMEM((2, RING, RING, RING, CAP, width), BF)
    dma = pltpu.SemaphoreType.DMA
    outs = pl.pallas_call(
        kernel,
        name="experts",
        out_shape=shapes,
        in_specs=[hbm, vmem, vmem, vmem] + [hbm] * 4,
        out_specs=(hbm, hbm, vmem, vmem, hbm, hbm, hbm),
        scratch_shapes=ring * 2 + plane * 2 + [full] * 4 + plane * 2 + ring * 2
        + [
            pltpu.VMEM((width, hidden), BF),
            pltpu.VMEM((width, hidden), BF),
            pltpu.VMEM((hidden, width), BF),
            pltpu.VMEM((DEV * CAP, hidden), BF),
            pltpu.VMEM((DEV * CAP, hidden), BF),
            pltpu.VMEM((DEV * CAP, hidden), BF),
            pltpu.VMEM((2, TILE, hidden), BF),
            pltpu.VMEM((2, TILE, hidden), BF),
            pltpu.VMEM((2, hidden, TILE), BF),
            pltpu.VMEM((GROUPS, RING, 8, tok), F32),
            pltpu.VMEM((GROUPS, 3, PLANE * CAP, RING * tok), BF),
            pltpu.VMEM((GROUPS, RING, 4, tok), F32),
            pltpu.VMEM((GROUPS, RING, 4, tok), F32),
            pltpu.VMEM((1, width), F32),
            pltpu.VMEM((16, 1, width), F32),
            pltpu.VMEM((8, 1, width), F32),
            pltpu.VMEM((tok, 1), F32),
        ]
        + [pltpu.VMEM((tok, width), BF)] * 3
        + [
            dma((3,)),
            dma((4, GROUPS)),
            dma((4, 2, GROUPS)),
            dma((3, 2)),
            dma((2,)),
            dma((2,)),
            dma((2, GROUPS)),
            dma((2, GROUPS, 3)),
            dma((2, GROUPS)),
            dma((2, GROUPS)),
            dma((2,)),
            dma((2,)),
            dma((GROUPS + 1,)),
            dma((GROUPS + 1,)),
        ],
        compiler_params=pltpu.CompilerParams(
            collective_id=0, has_side_effects=True, vmem_limit_bytes=65400 * 1024
        ),
    )(
        tokens, gain[None], expert_ids.T, gates.T, grad_out, w_gate[0], w_up[0], w_down[0],
    )
    steps = 4
    columns = pl.BlockSpec((tok, width // steps), lambda i: (0, i))
    weights = pl.BlockSpec((width // steps, hidden), lambda i: (i, 0))
    blocks = (
        columns, columns, pl.BlockSpec((4, tok), lambda i: (0, 0)),
        pl.BlockSpec((1, width // steps), lambda i: (0, i)),
        weights, weights, pl.BlockSpec((hidden // steps, width), lambda i: (i, 0)),
    )
    outs = pl.pallas_call(
        publish,
        name="publish",
        grid=(steps,),
        out_shape=shapes,
        in_specs=list(blocks),
        out_specs=blocks,
        compiler_params=pltpu.CompilerParams(vmem_limit_bytes=60 * 1024 * 1024),
    )(*outs)
    moe_out, token_gradient, grad_gates, gain_gradient, grad_gate, grad_up, grad_down = outs
    return (
        moe_out, token_gradient, grad_gates.T, gain_gradient[0],
        grad_gate[None], grad_up[None], grad_down[None],
    )


def solution(mesh):
    both = P(("dp", "expert"), None)
    three = P(("dp", "expert"), None, None)
    return jax.shard_map(
        body,
        mesh=mesh,
        in_specs=(both, P(), both, both, three, three, three, both),
        out_specs=(both, both, both, P(), three, three, three),
        check_vma=False,
    )
```
